256 devices in a mesh: seq: 16 (over y, x), head: 8 (over z), dp: 2 (over core).
Axes of the slice: x: 4, y: 4, z: 8, core: 2. Of those that a mesh axis runs over, the one named last changes fastest.
Arguments:
- hidden: bfloat16 [8192, 2560], P(('dp', 'seq', 'head')), parts along dimension 0, may hold values from -6 to 6
- x_input: bfloat16 [8192, 5120], P(('dp', 'seq', 'head')), parts along dimension 0, may hold values from -6 to 6
- grad_out: bfloat16 [8192, 5120], P(('dp', 'seq', 'head')), parts along dimension 0, may hold values from -6 to 6
- bc_weight: bfloat16 [2560, 256], replicated, may hold values from -0.01953125 to 0.01953125
- dt_weight: bfloat16 [2560, 80], replicated, may hold values from -0.125 to 0.125
- dt_bias: float32 [80], replicated, may hold values from -3 to -2
- a_log: float32 [80], replicated, may hold values from -10 to -1.6
- d_skip: float32 [80], replicated, may hold values from 0.5 to 1.5
Outputs:
- mixer_out: bfloat16 [8192, 5120], P(('dp', 'seq', 'head')), parts along dimension 0
- grad_x: bfloat16 [8192, 5120], P(('dp', 'seq', 'head')), parts along dimension 0
- grad_hidden: bfloat16 [8192, 2560], P(('dp', 'seq', 'head')), parts along dimension 0
- grad_bc_weight: float32 [5120, 256], P('dp'), parts along dimension 0
- grad_dt_weight: float32 [5120, 80], P('dp'), parts along dimension 0
- param_grads: float32 [6, 80], P('dp'), parts along dimension 0
The draws below stay inside these ranges and needn't reach their ends.
There are 2 independent parts, one for each index of `dp`. The reference program is written for one: setup_inputs(seed, part) draws one part's arguments, and reference() takes and returns one part's arrays. A program takes and returns all parts, laid end to end along the dimension named above; an argument that names none is the same for every part. Nothing has to cross between parts.
All inputs are finite; a program needn't handle non-finite values.
Results may differ from the reference program's by a relative error of at most 0.02.
Values may be sent and summed in bfloat16 or wider, within the bound.
No kernel may reach another device: no remote copies, remote signals or barrier semaphores. Data moves between devices by JAX's collectives and lax.ppermute only.
A program may use at most 128 MiB of HBM per device.

```python
import jax
import jax.numpy as jnp
from jax import lax

D = 2560
H = 80
P_SIZE = 64
N = 128
Q = 256
SEQLEN = 4096


def draw_a_log(key, part):
    first_key = jax.random.fold_in(key, 0)
    lowest = jnp.log(0.2 / SEQLEN)
    highest = jnp.log(1.0 / 40.0)
    spread = jax.random.uniform(first_key, (H,), jnp.float32)
    rates = lowest + spread * (highest - lowest)
    return (rates + 2.0).astype(jnp.float32)


def steps_of(stream_key, extent, shards, least, largest):
    factor_of = 1.0
    for position, parts in shards:
        steps = jax.random.uniform(jax.random.fold_in(jax.random.fold_in(stream_key, 6), position), (parts,), jnp.float32, least / len(shards), largest / len(shards))
        factor_of = factor_of * jnp.repeat(jnp.exp(steps), extent[position] // parts).reshape((-1,) + (1,) * (len(extent) - 1 - position))
    return factor_of


def centred(key, extent, deviation, reach, shards=(), kind=jnp.bfloat16):
    drawn = jax.random.normal(key, extent, jnp.float32) * deviation
    if len(shards) > 0:
        drawn = steps_of(key, extent, shards, -0.22, 0.18) * drawn
    return jnp.clip(drawn, min=-reach, max=reach).astype(kind)


def setup_inputs(seed: int = 0, part: int = 0) -> dict:
    keys = jax.random.split(jax.random.key(seed), 9)
    part_splits = jax.random.split(jax.random.fold_in(keys[8], part), 9)
    return {
        "hidden": centred(part_splits[0], (SEQLEN, D), 1.0, 6.0, ((0, 128),)),
        "x_input": centred(part_splits[1], (SEQLEN, H * P_SIZE), 1.0, 6.0, ((0, 128),)),
        "grad_out": centred(part_splits[2], (SEQLEN, H * P_SIZE), 1.0, 6.0, ((0, 128),)),
        "bc_weight": centred(keys[3], (D, 2 * N), (0.17 * D ** -0.5), 0.01953125),
        "dt_weight": centred(keys[4], (D, H), D ** -0.5, 0.125),
        "dt_bias": jnp.clip(jax.random.uniform(keys[5], (H,), jnp.float32, -3.0, -2.0), -3.0, -2.0),
        "a_log": draw_a_log(jax.random.fold_in(keys[8], 71), part),
        "d_skip": jnp.clip(jax.random.uniform(keys[7], (H,), jnp.float32, 0.5, 1.5), 0.5, 1.5),
    }


precise = lax.Precision.HIGHEST

def span_scan(x_heads, step_size, b_rows, c_rows, neg_rate, state_in):
    length = x_heads.shape[0]
    blocks = length // Q
    heads_here = x_heads.shape[1]
    head_width = x_heads.shape[2]
    states = b_rows.shape[1]
    causal = (jnp.arange(Q)[:, None] >= jnp.arange(Q)[None, :])[:, :, None]

    def advance(carry, block):
        x_block, step_block, b_block, c_block = block
        running = jnp.cumsum(step_block * neg_rate[None, :], axis=0)
        scores = jnp.dot(c_block, b_block.T, precision=precise)
        spread = running[:, None, :] - running[None, :, :]
        decay = jnp.where(causal, jnp.exp(jnp.where(causal, spread, 0.0)), 0.0)
        scaled_x = x_block * step_block[:, :, None]
        inner = jnp.einsum('qkh,khp->qhp', decay * scores[:, :, None], scaled_x, precision=precise)
        carried = jnp.einsum('qn,hnp->qhp', c_block, carry, precision=precise) * jnp.exp(running)[:, :, None]
        total = running[-1]
        weights_end = jnp.exp(total[None, :] - running)
        fresh = jnp.einsum('kn,khp->hnp', b_block, scaled_x * weights_end[:, :, None], precision=precise)
        return (jnp.exp(total)[:, None, None] * carry + fresh, inner + carried)
    pieces = (x_heads.reshape(blocks, Q, heads_here, head_width), step_size.reshape(blocks, Q, heads_here), b_rows.reshape(blocks, Q, states), c_rows.reshape(blocks, Q, states))
    state_out, outputs = lax.scan(jax.checkpoint(advance), state_in, pieces)
    return (outputs.reshape(length, heads_here, head_width), state_out)

def mixer_local(x_heads, raw_step, b_rows, c_rows, log_decay, skip_gain, step_bias, state_in):
    step_size = jax.nn.softplus(raw_step + step_bias[None, :])
    neg_rate = -jnp.exp(log_decay)
    mixed, state_out = span_scan(x_heads, step_size, b_rows, c_rows, neg_rate, state_in)
    return (mixed + skip_gain[None, :, None] * x_heads, state_out)

def reference(hidden, x_input, grad_out, bc_weight, dt_weight, dt_bias, a_log, d_skip):
    proj_bc = jnp.dot(hidden, bc_weight, preferred_element_type=jnp.float32).astype(jnp.bfloat16)
    proj_dt = jnp.dot(hidden, dt_weight, preferred_element_type=jnp.float32).astype(jnp.bfloat16)
    x_heads = x_input.astype(jnp.float32).reshape(SEQLEN, H, P_SIZE)
    raw_step = proj_dt.astype(jnp.float32)
    b_rows = proj_bc[:, :N].astype(jnp.float32)
    c_rows = proj_bc[:, N:].astype(jnp.float32)
    state_zero = jnp.zeros((H, N, P_SIZE), jnp.float32)

    def forward(x_arg, raw_arg, b_arg, c_arg, log_arg, skip_arg, bias_arg):
        return mixer_local(x_arg, raw_arg, b_arg, c_arg, log_arg, skip_arg, bias_arg, state_zero)
    (mixed, state_end), pullback = jax.vjp(forward, x_heads, raw_step, b_rows, c_rows, a_log, d_skip, dt_bias)
    cotangent = (grad_out.astype(jnp.float32).reshape(SEQLEN, H, P_SIZE), jnp.zeros_like(state_end))
    grad_xs, grad_raw, grad_b, grad_c, grad_alog, grad_skip, grad_bias = pullback(cotangent)
    mixer_out = mixed.reshape(SEQLEN, H * P_SIZE).astype(jnp.bfloat16)
    grad_x = grad_xs.reshape(SEQLEN, H * P_SIZE).astype(jnp.bfloat16)
    d_bc = jnp.concatenate([grad_b, grad_c], axis=1).astype(jnp.bfloat16)
    d_step = grad_raw.astype(jnp.bfloat16)
    grad_hidden = (jnp.dot(d_bc, bc_weight.T, preferred_element_type=jnp.float32) + jnp.dot(d_step, dt_weight.T, preferred_element_type=jnp.float32)).astype(jnp.bfloat16)
    grad_bc_weight = jnp.dot(hidden.T, d_bc, preferred_element_type=jnp.float32) / SEQLEN
    grad_dt_weight = jnp.dot(hidden.T, d_step, preferred_element_type=jnp.float32) / SEQLEN
    param_grads = jnp.stack([grad_bias, grad_alog, grad_skip]) / SEQLEN
    return (mixer_out, grad_x, grad_hidden, grad_bc_weight, grad_dt_weight, param_grads)
```

```python
import functools

import jax
import jax.numpy as jnp
from jax import lax
from jax.experimental import pallas as pl
from jax.experimental.pallas import tpu as pltpu
from jax.sharding import PartitionSpec as P

F32 = jnp.float32
BF16 = jnp.bfloat16
LANES = 128
LIMIT = 48 * 2**20

SEQ, HEAD = 16, 8
D, H, WIDTH, N = 2560, 80, 64, 128
TOKENS = 32
SPAN = TOKENS * HEAD
HEADS = H // HEAD
CH = HEADS * WIDTH
TOTAL = SPAN * SEQ
COLS = D // SEQ
PACK = 2 * CH + 2 * N + LANES
DPACK = 2 * N + LANES
SLAB = N // SEQ
STEP = 2 * CH + 2 * N


def dot(a, b, ca=1, cb=0):
    return lax.dot_general(a, b, (((ca,), (cb,)), ((), ())), preferred_element_type=F32)


def iota(shape, dim):
    return lax.broadcasted_iota(jnp.int32, shape, dim)


def split(v, parts):
    out = []
    for _ in range(parts):
        top = v.astype(BF16)
        out.append(top)
        v = v - top.astype(F32)
    return out


def one_hot(shift=0):
    return (iota((LANES, CH), 0) - shift == iota((LANES, CH), 1) // WIDTH).astype(F32).astype(BF16)


def spread(v, hot):
    hi, lo = split(v, 2)
    return dot(hi, hot) + dot(lo, hot)


def gather_heads(v, hot, parts=2):
    return sum(dot(part, hot, 1, 1) for part in split(v, parts))


def triangle(dim):
    return (iota((SPAN, SPAN), dim) >= iota((SPAN, SPAN), 1 - dim)).astype(F32).astype(BF16)


def running_sum(tri, v):
    return sum(dot(tri, part) for part in split(v, 3))


def head_params(prm_ref):
    prm = pltpu.roll(prm_ref[...], lax.rem(LANES - HEADS * lax.axis_index("head"), LANES), 1)
    return prm[0:1], -jnp.exp(prm[1:2]), prm[2:3]


def step_sizes(r_ref, prm_ref):
    bias, rate, skip = head_params(prm_ref)
    pre = r_ref[:, STEP:].astype(F32) + bias
    step = jnp.maximum(pre, 0.0) + jnp.log1p(jnp.exp(-jnp.abs(pre)))
    cum = running_sum(triangle(0), step * rate)
    return pre, step, cum, rate, skip


def project_kernel(hid_ref, wbc_ref, wdt_ref, x_ref, g_ref, send_ref, hs_ref):
    hid = hid_ref[...]
    bc = dot(hid, wbc_ref[...]).astype(BF16)
    raw = dot(hid, wdt_ref[...]).astype(BF16).astype(F32)
    raw = jnp.concatenate([raw, jnp.zeros((TOKENS, LANES - H), F32)], axis=1)
    lane = iota((TOKENS, LANES), 1)
    for k in range(HEAD):
        send_ref[k, :, :CH] = x_ref[:, k * CH : (k + 1) * CH]
        send_ref[k, :, CH : 2 * CH] = g_ref[:, k * CH : (k + 1) * CH]
        send_ref[k, :, 2 * CH : STEP] = bc
        mine = pltpu.roll(raw, (LANES - HEADS * k) % LANES, 1)
        send_ref[k, :, STEP:] = jnp.where(lane < HEADS, mine, 0.0).astype(BF16)
    half = TOKENS // 2
    wide = hid.astype(F32)
    pad = jnp.zeros((half, 3 * LANES - 2 * COLS), F32)
    for s in range(SEQ):
        part = wide[:, s * COLS : (s + 1) * COLS]
        hs_ref[s] = jnp.concatenate([part[:half], part[half:], pad], axis=1).astype(BF16)


def totals_kernel(r_ref, prm_ref, hs_ref, send_ref):
    pre, step, cum, rate, skip = step_sizes(r_ref, prm_ref)
    hot = one_hot()
    total = cum[SPAN - 1 :]
    to_end = spread(step * jnp.exp(total - cum), hot)
    from_start = spread(jnp.exp(cum), hot)
    x = r_ref[:, :CH].astype(F32)
    g = r_ref[:, CH : 2 * CH].astype(F32)
    b = r_ref[:, 2 * CH : 2 * CH + N]
    c = r_ref[:, 2 * CH + N : STEP]
    fresh = dot(b, (x * to_end).astype(BF16), 0, 0)
    back = dot(c, (g * from_start).astype(BF16), 0, 0)
    both = jnp.concatenate(
        [fresh.reshape(SEQ, SLAB, CH), back.reshape(SEQ, SLAB, CH)], axis=1
    )
    send_ref[:, :, :CH] = both.astype(BF16)
    hi, lo = split(jnp.exp(total), 2)
    row = iota((2 * SLAB, LANES), 0)
    lane = iota((2 * SLAB, LANES), 1)
    decay = jnp.where(row == 0, hi.astype(F32), jnp.where(row == 1, lo.astype(F32), 0.0))
    decay = pltpu.roll(jnp.where(lane < HEADS, decay, 0.0), WIDTH, 1)
    send_ref[:, :, CH : CH + 2 * LANES] = hs_ref[:, :, : 2 * LANES]
    tail = hs_ref[:, :, 2 * LANES :].astype(F32) + decay[None]
    send_ref[:, :, CH + 2 * LANES :] = tail.astype(BF16)


def prefix_kernel(r_ref, out_ref):
    hot = one_hot(WIDTH)
    tail = r_ref[:, :, CH + 2 * LANES :].astype(F32)
    decay = dot(tail[:, 0, :].astype(BF16), hot) + dot(tail[:, 1, :].astype(BF16), hot)
    ahead, behind = [], [None] * SEQ
    state = jnp.zeros((SLAB, CH), F32)
    for s in range(SEQ):
        ahead.append(state)
        state = decay[s : s + 1] * state + r_ref[s, :, :CH].astype(F32)[:SLAB]
    state = jnp.zeros((SLAB, CH), F32)
    for s in reversed(range(SEQ)):
        behind[s] = state
        state = decay[s : s + 1] * state + r_ref[s, :, :CH].astype(F32)[SLAB:]
    for s in range(SEQ):
        out_ref[s] = jnp.concatenate([ahead[s], behind[s]], axis=0).astype(BF16)


def inner_kernel(r_ref, prm_ref, y_ref, du_ref, db_ref, dc_ref, e_ref, ds_ref):
    pre, step, cum, rate, skip = step_sizes(r_ref, prm_ref)
    hot = one_hot()
    cum_t = cum.T
    b = r_ref[:, 2 * CH : 2 * CH + N]
    c = r_ref[:, 2 * CH + N : STEP]
    scores = dot(c, b, 1, 1)
    causal = iota((SPAN, SPAN), 0) >= iota((SPAN, SPAN), 1)
    step_x = spread(step, hot)
    low = iota((SPAN, LANES), 1) < WIDTH
    zero = jnp.zeros((SPAN, LANES), BF16)
    products = []
    for j in range(HEADS // 2):
        at = slice(j * LANES, (j + 1) * LANES)
        g = r_ref[:, CH + j * LANES : CH + (j + 1) * LANES]
        u = (r_ref[:, at].astype(F32) * step_x[:, at]).astype(BF16)
        g_t = g.astype(F32).T.astype(BF16)
        y = jnp.zeros((SPAN, LANES), F32)
        du_t = []
        for i in range(2):
            h = 2 * j + i
            mine = low if i == 0 else jnp.logical_not(low)
            gap = jnp.where(causal, cum[:, h : h + 1] - cum_t[h : h + 1, :], -1e30)
            decay = jnp.exp(gap)
            mixer = (decay * scores).astype(BF16)
            y += dot(mixer, jnp.where(mine, u, zero))
            du_t.append(dot(g_t[i * WIDTH : (i + 1) * WIDTH], mixer))
            d_mixer = dot(jnp.where(mine, g, zero), u, 1, 1) * decay
            if h == 0:
                ds_ref[...] = d_mixer
            else:
                ds_ref[...] += d_mixer
        du = jnp.concatenate(du_t, axis=0).T
        y_ref[:, at] = y
        du_ref[:, at] = du
        products.append(g.astype(F32) * y - u.astype(F32) * du)
    e_ref[...] = gather_heads(jnp.concatenate(products, axis=1), hot, 3)
    ds = ds_ref[...]
    dc_ref[...] = dot(ds.astype(BF16), b)
    db_ref[...] = dot(ds.T.astype(BF16), c)


def carry_kernel(r_ref, prm_ref, st_ref, y_ref, du_ref, db_ref, dc_ref, e_ref, send_ref):
    pre, step, cum, rate, skip = step_sizes(r_ref, prm_ref)
    hot = one_hot()
    total = cum[SPAN - 1 :]
    step_x = spread(step, hot)
    to_end = spread(jnp.exp(total - cum), hot)
    from_start = spread(jnp.exp(cum), hot)
    skip_x = spread(jnp.broadcast_to(skip, (8, LANES)), hot)[:1]
    states = st_ref[...].astype(F32)
    state_in = states[:, :SLAB].reshape(N, CH)
    state_gr = states[:, SLAB:].reshape(N, CH)
    x = r_ref[:, :CH].astype(F32)
    g = r_ref[:, CH : 2 * CH].astype(F32)
    b = r_ref[:, 2 * CH : 2 * CH + N]
    c = r_ref[:, 2 * CH + N : STEP]
    s_b = state_in.astype(BF16)
    q_b = state_gr.astype(BF16)
    u = x * step_x
    carried = dot(c, s_b) * from_start
    late = dot(b, q_b) * to_end
    y = y_ref[...] + carried + skip_x * x
    du = du_ref[...] + late
    gx = step_x * du + skip_x * g
    d_c = dc_ref[...] + dot((g * from_start).astype(BF16), s_b, 1, 1)
    d_b = db_ref[...] + dot((u * to_end).astype(BF16), q_b, 1, 1)
    e = e_ref[...] + gather_heads(g * carried, hot)
    f = gather_heads(u * late, hot)
    xdu = gather_heads(x * du, hot)
    sums = jnp.concatenate(
        [
            jnp.sum(state_in * state_gr, axis=0, keepdims=True),
            jnp.sum(g * x, axis=0, keepdims=True),
            jnp.zeros((6, CH), F32),
        ],
        axis=0,
    )
    sums = gather_heads(sums, hot, 3)
    edge = jnp.exp(total) * sums[0:1]
    d_rate = running_sum(triangle(1), e) + running_sum(triangle(0), f) - f + edge
    d_raw = (rate * d_rate + xdu) / (1.0 + jnp.exp(-pre))
    d_bias = jnp.sum(d_raw, axis=0, keepdims=True)
    d_log = rate * jnp.sum(step * d_rate, axis=0, keepdims=True)
    hi, lo = split(jnp.concatenate([d_bias, d_log, sums[1:2]], axis=0), 2)
    row = jnp.concatenate(
        [hi.astype(F32), lo.astype(F32), jnp.zeros((TOKENS - 6, LANES), F32)], axis=0
    )
    lane = iota((TOKENS, LANES), 1)
    row = pltpu.roll(jnp.where(lane < HEADS, row, 0.0), 16, 1)
    for k in range(HEAD):
        at = slice(k * TOKENS, (k + 1) * TOKENS)
        send_ref[k, :, :CH] = y[at].astype(BF16)
        send_ref[k, :, CH : 2 * CH] = gx[at].astype(BF16)
        send_ref[k, :, 2 * CH : 2 * CH + N] = d_b[at].astype(BF16)
        send_ref[k, :, 2 * CH + N : STEP] = d_c[at].astype(BF16)
        send_ref[k, :, STEP:] = (jnp.where(lane < HEADS, d_raw[at], 0.0) + row).astype(BF16)


def reduce_kernel(r_ref, send_ref):
    d_bc = jnp.sum(r_ref[:, :, 2 * CH : STEP].astype(F32), axis=0).astype(BF16)
    lane = iota((TOKENS, LANES), 1)
    steps = jnp.zeros((TOKENS, LANES), F32)
    rows = [[], []]
    low = iota((8, LANES), 1)
    for k in range(HEAD):
        tile = r_ref[k, :, STEP:].astype(F32)
        steps += pltpu.roll(jnp.where(lane < HEADS, tile, 0.0), HEADS * k, 1)
        mine = jnp.where(jnp.logical_and(low >= 16, low < 16 + HEADS), tile[:8], 0.0)
        rows[k // 4].append(pltpu.roll(mine, H - 16 if k < 4 else H, 1))
    tail = steps + jnp.concatenate(rows[0], axis=0) + jnp.concatenate(rows[1], axis=0)
    tail = tail.astype(BF16)
    for s in range(SEQ):
        send_ref[s, :, : 2 * N] = d_bc
        send_ref[s, :, 2 * N :] = tail


def finish_kernel(r_ref, d_ref, wbc_ref, wdt_ref, y_ref, gx_ref, gh_ref):
    for k in range(HEAD):
        y_ref[:, k * CH : (k + 1) * CH] = r_ref[k, :, :CH]
        gx_ref[:, k * CH : (k + 1) * CH] = r_ref[k, :, CH : 2 * CH]
    d_bc = d_ref[0, :, : 2 * N]
    d_step = d_ref[0, :, 2 * N :][:, :H]
    gh = dot(d_bc, wbc_ref[...], 1, 1) + dot(d_step, wdt_ref[...], 1, 1)
    gh_ref[...] = gh.astype(BF16)


def weight_kernel(d_ref, h_ref, send_ref, par_ref):
    half = TOKENS // 2
    d = d_ref[...]
    h = h_ref[:, :, CH:].astype(F32)
    grad = jnp.zeros((COLS, DPACK), F32)
    for i in range(2):
        rows = h[:, :, i * COLS : (i + 1) * COLS].reshape(SEQ * half, COLS).astype(BF16)
        grad += dot(rows, d[:, i * half : (i + 1) * half].reshape(SEQ * half, DPACK), 0, 0)
    grad = grad.astype(BF16)
    for k in range(HEAD):
        send_ref[k] = grad
    tail = jnp.sum(d[:, :, 2 * N :].astype(F32), axis=0)
    low = iota((8, LANES), 1)
    out = jnp.zeros((8, LANES), F32)
    for k in range(HEAD):
        at = H if k < 4 else H + 16
        rolled = pltpu.roll(tail[8 * (k % 4) : 8 * (k % 4) + 8], (HEADS * k - at) % LANES, 1)
        mine = jnp.logical_and(low >= HEADS * k, low < HEADS * (k + 1))
        out += jnp.where(mine, rolled, 0.0)
    par_ref[...] = ((out[0:3] + out[3:6]) / TOTAL)[:, :H]


def sum_kernel(r_ref, send_ref):
    grad = (jnp.sum(r_ref[...].astype(F32), axis=0) / TOTAL).astype(BF16)
    for s in range(SEQ):
        send_ref[s] = grad


def unpack_kernel(r_ref, bc_ref, dt_ref):
    for s in range(r_ref.shape[0]):
        at = slice(s * COLS, (s + 1) * COLS)
        bc_ref[at, :] = r_ref[s, :, : 2 * N].astype(F32)
        dt_ref[at, :] = r_ref[s, :, 2 * N :].astype(F32)[:, :H]


def call(kernel, outs, *args, scratch=()):
    return pl.pallas_call(
        kernel,
        out_shape=[jax.ShapeDtypeStruct(shape, kind) for shape, kind in outs],
        in_specs=[pl.BlockSpec(memory_space=pltpu.VMEM)] * len(args),
        out_specs=[pl.BlockSpec(memory_space=pltpu.VMEM)] * len(outs),
        scratch_shapes=list(scratch),
        compiler_params=pltpu.CompilerParams(vmem_limit_bytes=LIMIT),
    )(*args)


def exchange(v, axis):
    return lax.all_to_all(v, axis, split_axis=0, concat_axis=0, tiled=True)


def per_device(hidden, x_input, grad_out, bc_weight, dt_weight, dt_bias, a_log, d_skip):
    prm = jnp.pad(jnp.stack([dt_bias, a_log, d_skip]), ((0, 5), (0, LANES - H)))
    packed, hid_send = call(
        project_kernel,
        [((HEAD, TOKENS, PACK), BF16), ((SEQ, TOKENS // 2, 3 * LANES), BF16)],
        hidden, bc_weight, dt_weight, x_input, grad_out,
    )
    mine = exchange(packed, "head").reshape(SPAN, PACK)
    [sent] = call(
        totals_kernel, [((SEQ, 2 * SLAB, CH + 3 * LANES), BF16)], mine, prm, hid_send
    )
    totals = exchange(sent, "seq")
    y, du, db, dc, e = call(
        inner_kernel,
        [((SPAN, CH), F32), ((SPAN, CH), F32), ((SPAN, N), F32), ((SPAN, N), F32), ((SPAN, LANES), F32)],
        mine, prm,
        scratch=[pltpu.VMEM((SPAN, SPAN), F32)],
    )
    [states] = call(prefix_kernel, [((SEQ, 2 * SLAB, CH), BF16)], totals)
    states = exchange(states, "seq")
    [results] = call(
        carry_kernel, [((HEAD, TOKENS, PACK), BF16)], mine, prm, states, y, du, db, dc, e
    )
    results = exchange(results, "head")
    [d_send] = call(reduce_kernel, [((SEQ, TOKENS, DPACK), BF16)], results)
    d_all = exchange(d_send, "seq")
    mixer_out, grad_x, grad_hidden = call(
        finish_kernel,
        [((TOKENS, H * WIDTH), BF16), ((TOKENS, H * WIDTH), BF16), ((TOKENS, D), BF16)],
        results, d_send, bc_weight, dt_weight,
    )
    w_send, param_grads = call(
        weight_kernel, [((HEAD, COLS, DPACK), BF16), ((3, H), F32)], d_all, totals
    )
    w_parts = exchange(w_send, "head")
    [w_sum] = call(sum_kernel, [((SEQ, COLS, DPACK), BF16)], w_parts)
    w_all = exchange(w_sum, "seq")
    grad_bc_weight, grad_dt_weight = call(
        unpack_kernel, [((D, 2 * N), F32), ((D, H), F32)], w_all
    )
    return (mixer_out, grad_x, grad_hidden, grad_bc_weight, grad_dt_weight, param_grads)


def solution(mesh):
    rows = P(("dp", "seq", "head"), None)
    return jax.shard_map(
        per_device,
        mesh=mesh,
        in_specs=(rows, rows, rows, P(), P(), P(), P(), P()),
        out_specs=(rows, rows, rows, P("dp", None), P("dp", None), P("dp", None)),
        check_vma=False,
    )
```

```python
import functools

import jax
import jax.numpy as jnp
from jax import lax
from jax.experimental import pallas as pl
from jax.experimental.pallas import tpu as pltpu
from jax.sharding import PartitionSpec as P

F32 = jnp.float32
BF16 = jnp.bfloat16
LANES = 128
LIMIT = 24 * 2**20
FULL = 60 * 2**20

SEQ, HEAD = 16, 8
D, H, WIDTH, N = 2560, 80, 64, 128
TOKENS = 32
SPAN = TOKENS * HEAD
HEADS = H // HEAD
CH = HEADS * WIDTH
TOTAL = SPAN * SEQ
COLS = D // SEQ
PACK = 2 * CH + 2 * N + LANES
DPACK = 2 * N + LANES
STAGES = 4
SLAB = N // SEQ
STEP = 2 * CH + 2 * N


def dot(a, b, ca=1, cb=0):
    return lax.dot_general(a, b, (((ca,), (cb,)), ((), ())), preferred_element_type=F32)


def iota(shape, dim):
    return lax.broadcasted_iota(jnp.int32, shape, dim)


def split(v, parts):
    out = []
    for _ in range(parts):
        top = v.astype(BF16)
        out.append(top)
        v = v - top.astype(F32)
    return out


def one_hot(shift=0):
    return (iota((LANES, CH), 0) - shift == iota((LANES, CH), 1) // WIDTH).astype(F32).astype(BF16)


def spread(v, hot):
    hi, lo = split(v, 2)
    return dot(hi, hot) + dot(lo, hot)


def gather_heads(v, hot, parts=2):
    return sum(dot(part, hot, 1, 1) for part in split(v, parts))


def triangle(dim):
    return (iota((SPAN, SPAN), dim) >= iota((SPAN, SPAN), 1 - dim)).astype(F32).astype(BF16)


def running_sum(tri, v):
    return sum(dot(tri, part) for part in split(v, 3))


def head_params(prm_ref):
    prm = pltpu.roll(prm_ref[...], lax.rem(LANES - HEADS * lax.axis_index("head"), LANES), 1)
    return prm[0:1], -jnp.exp(prm[1:2]), prm[2:3]


def step_sizes(r_ref, prm_ref):
    bias, rate, skip = head_params(prm_ref)
    pre = r_ref[:, STEP:].astype(F32) + bias
    step = jnp.maximum(pre, 0.0) + jnp.log1p(jnp.exp(-jnp.abs(pre)))
    cum = running_sum(triangle(0), step * rate)
    return pre, step, cum, rate, skip


def project_kernel(
    hid_hbm, wbc_hbm, wdt_hbm, x_hbm, g_hbm, send_ref, hid_ref, wbc_ref, wdt_ref, sems
):
    first = [
        pltpu.make_async_copy(hid_hbm, hid_ref, sems.at[0]),
        pltpu.make_async_copy(wdt_hbm, wdt_ref, sems.at[1]),
        pltpu.make_async_copy(wbc_hbm, wbc_ref, sems.at[2]),
    ]
    rest = []
    for k in range(HEAD):
        for i, ref in enumerate((x_hbm, g_hbm)):
            rest.append(
                pltpu.make_async_copy(
                    ref.at[:, k * CH : (k + 1) * CH],
                    send_ref.at[k, :, i * CH : (i + 1) * CH],
                    sems.at[3 + 2 * k + i],
                )
            )
    for copy in first + rest:
        copy.start()
    first[0].wait()
    hid = hid_ref[...]
    first[1].wait()
    raw = dot(hid, wdt_ref[...], 1, 1).astype(BF16).astype(F32)
    raw = jnp.concatenate([raw, jnp.zeros((TOKENS, LANES - H), F32)], axis=1)
    first[2].wait()
    bc = dot(hid, wbc_ref[...]).astype(BF16)
    lane = iota((TOKENS, LANES), 1)
    for k in range(HEAD):
        send_ref[k, :, 2 * CH : STEP] = bc
        mine = pltpu.roll(raw, (LANES - HEADS * k) % LANES, 1)
        send_ref[k, :, STEP:] = jnp.where(lane < HEADS, mine, 0.0).astype(BF16)
    for copy in rest:
        copy.wait()


def slab_kernel(hid_ref, hs_ref):
    half = TOKENS // 2
    wide = hid_ref[...].astype(F32)
    pad = jnp.zeros((half, 3 * LANES - 2 * COLS), F32)
    for s in range(SEQ):
        part = wide[:, s * COLS : (s + 1) * COLS]
        hs_ref[s] = jnp.concatenate([part[:half], part[half:], pad], axis=1).astype(BF16)


def totals_kernel(r_ref, prm_ref, hs_ref, send_ref):
    pre, step, cum, rate, skip = step_sizes(r_ref, prm_ref)
    hot = one_hot()
    total = cum[SPAN - 1 :]
    to_end = spread(step * jnp.exp(total - cum), hot)
    from_start = spread(jnp.exp(cum), hot)
    x = r_ref[:, :CH].astype(F32)
    g = r_ref[:, CH : 2 * CH].astype(F32)
    b = r_ref[:, 2 * CH : 2 * CH + N]
    c = r_ref[:, 2 * CH + N : STEP]
    fresh = dot(b, (x * to_end).astype(BF16), 0, 0)
    back = dot(c, (g * from_start).astype(BF16), 0, 0)
    both = jnp.concatenate(
        [fresh.reshape(SEQ, SLAB, CH), back.reshape(SEQ, SLAB, CH)], axis=1
    )
    send_ref[:, :, :CH] = both.astype(BF16)
    hi, lo = split(jnp.exp(total), 2)
    row = iota((2 * SLAB, LANES), 0)
    lane = iota((2 * SLAB, LANES), 1)
    decay = jnp.where(row == 0, hi.astype(F32), jnp.where(row == 1, lo.astype(F32), 0.0))
    decay = pltpu.roll(jnp.where(lane < HEADS, decay, 0.0), WIDTH, 1)
    send_ref[:, :, CH : CH + 2 * LANES] = hs_ref[:, :, : 2 * LANES]
    tail = hs_ref[:, :, 2 * LANES :].astype(F32) + decay[None]
    send_ref[:, :, CH + 2 * LANES :] = tail.astype(BF16)


def prefix_kernel(r_ref, out_ref):
    hot = one_hot(WIDTH)
    tail = r_ref[:, :, CH + 2 * LANES :].astype(F32)
    decay = dot(tail[:, 0, :].astype(BF16), hot) + dot(tail[:, 1, :].astype(BF16), hot)
    ahead, behind = [], [None] * SEQ
    state = jnp.zeros((SLAB, CH), F32)
    for s in range(SEQ):
        ahead.append(state)
        state = decay[s : s + 1] * state + r_ref[s, :, :CH].astype(F32)[:SLAB]
    state = jnp.zeros((SLAB, CH), F32)
    for s in reversed(range(SEQ)):
        behind[s] = state
        state = decay[s : s + 1] * state + r_ref[s, :, :CH].astype(F32)[SLAB:]
    for s in range(SEQ):
        out_ref[s] = jnp.concatenate([ahead[s], behind[s]], axis=0).astype(BF16)


def inner_kernel(r_ref, prm_ref, out_ref, ds_ref):
    pre, step, cum, rate, skip = step_sizes(r_ref, prm_ref)
    hot = one_hot()
    cum_t = cum.T
    b = r_ref[:, 2 * CH : 2 * CH + N]
    c = r_ref[:, 2 * CH + N : STEP]
    scores = dot(c, b, 1, 1)
    causal = iota((SPAN, SPAN), 0) >= iota((SPAN, SPAN), 1)
    step_x = spread(step, hot)
    low = iota((SPAN, LANES), 1) < WIDTH
    zero = jnp.zeros((SPAN, LANES), BF16)
    products = []
    for j in range(HEADS // 2):
        at = slice(j * LANES, (j + 1) * LANES)
        g = r_ref[:, CH + j * LANES : CH + (j + 1) * LANES]
        u = (r_ref[:, at].astype(F32) * step_x[:, at]).astype(BF16)
        g_t = g.astype(F32).T.astype(BF16)
        y = jnp.zeros((SPAN, LANES), F32)
        du_t = []
        for i in range(2):
            h = 2 * j + i
            mine = low if i == 0 else jnp.logical_not(low)
            gap = jnp.where(causal, cum[:, h : h + 1] - cum_t[h : h + 1, :], -1e30)
            decay = jnp.exp(gap)
            mixer = (decay * scores).astype(BF16)
            y += dot(mixer, jnp.where(mine, u, zero))
            du_t.append(dot(g_t[i * WIDTH : (i + 1) * WIDTH], mixer))
            d_mixer = dot(jnp.where(mine, g, zero), u, 1, 1) * decay
            if h == 0:
                ds_ref[...] = d_mixer
            else:
                ds_ref[...] += d_mixer
        du = jnp.concatenate(du_t, axis=0).T
        out_ref[:, at] = y
        out_ref[:, CH + j * LANES : CH + (j + 1) * LANES] = du
        products.append(g.astype(F32) * y - u.astype(F32) * du)
    out_ref[:, STEP:] = gather_heads(jnp.concatenate(products, axis=1), hot, 3)
    ds = ds_ref[...]
    out_ref[:, 2 * CH : 2 * CH + N] = dot(ds.T.astype(BF16), c)
    out_ref[:, 2 * CH + N : STEP] = dot(ds.astype(BF16), b)


def carry_kernel(r_ref, prm_ref, st_ref, in_ref, send_ref, both_ref):
    pre, step, cum, rate, skip = step_sizes(r_ref, prm_ref)
    hot = one_hot()
    total = cum[SPAN - 1 :]
    step_x = spread(step, hot)
    to_end = spread(jnp.exp(total - cum), hot)
    from_start = spread(jnp.exp(cum), hot)
    skip_x = spread(jnp.broadcast_to(skip, (8, LANES)), hot)[:1]
    states = st_ref[...].astype(F32)
    state_in = states[:, :SLAB].reshape(N, CH)
    state_gr = states[:, SLAB:].reshape(N, CH)
    x = r_ref[:, :CH].astype(F32)
    g = r_ref[:, CH : 2 * CH].astype(F32)
    b = r_ref[:, 2 * CH : 2 * CH + N]
    c = r_ref[:, 2 * CH + N : STEP]
    s_b = state_in.astype(BF16)
    q_b = state_gr.astype(BF16)
    u = x * step_x
    carried = dot(c, s_b) * from_start
    late = dot(b, q_b) * to_end
    y = in_ref[:, :CH] + carried + skip_x * x
    du = in_ref[:, CH : 2 * CH] + late
    gx = step_x * du + skip_x * g
    d_c = in_ref[:, 2 * CH + N : STEP] + dot((g * from_start).astype(BF16), s_b, 1, 1)
    d_b = in_ref[:, 2 * CH : 2 * CH + N] + dot((u * to_end).astype(BF16), q_b, 1, 1)
    e = in_ref[:, STEP:] + gather_heads(g * carried, hot)
    f = gather_heads(u * late, hot)
    xdu = gather_heads(x * du, hot)
    sums = jnp.concatenate(
        [
            jnp.sum(state_in * state_gr, axis=0, keepdims=True),
            jnp.sum(g * x, axis=0, keepdims=True),
            jnp.zeros((6, CH), F32),
        ],
        axis=0,
    )
    sums = gather_heads(sums, hot, 3)
    edge = jnp.exp(total) * sums[0:1]
    d_rate = running_sum(triangle(1), e) + running_sum(triangle(0), f) - f + edge
    d_raw = (rate * d_rate + xdu) / (1.0 + jnp.exp(-pre))
    d_bias = jnp.sum(d_raw, axis=0, keepdims=True)
    d_log = rate * jnp.sum(step * d_rate, axis=0, keepdims=True)
    hi, lo = split(jnp.concatenate([d_bias, d_log, sums[1:2]], axis=0), 2)
    row = jnp.concatenate(
        [hi.astype(F32), lo.astype(F32), jnp.zeros((TOKENS - 6, LANES), F32)], axis=0
    )
    lane = iota((TOKENS, LANES), 1)
    row = pltpu.roll(jnp.where(lane < HEADS, row, 0.0), 16, 1)
    both_ref[:, :CH] = y.astype(BF16)
    both_ref[:, CH:] = gx.astype(BF16)
    for k in range(HEAD):
        at = slice(k * TOKENS, (k + 1) * TOKENS)
        send_ref[k, :, :N] = d_b[at].astype(BF16)
        send_ref[k, :, N : 2 * N] = d_c[at].astype(BF16)
        send_ref[k, :, 2 * N :] = (jnp.where(lane < HEADS, d_raw[at], 0.0) + row).astype(BF16)


def rotate_kernel(both_ref, *blocks):
    for k in range(HEAD):
        to = lax.rem(lax.axis_index("head") + k, HEAD)
        blocks[k][...] = both_ref[pl.ds(pl.multiple_of(to * TOKENS, TOKENS), TOKENS), :]


def reduce_kernel(r_ref, send_ref):
    d_bc = jnp.sum(r_ref[:, :, : 2 * N].astype(F32), axis=0).astype(BF16)
    lane = iota((TOKENS, LANES), 1)
    steps = jnp.zeros((TOKENS, LANES), F32)
    rows = [[], []]
    low = iota((8, LANES), 1)
    for k in range(HEAD):
        tile = r_ref[k, :, 2 * N :].astype(F32)
        steps += pltpu.roll(jnp.where(lane < HEADS, tile, 0.0), HEADS * k, 1)
        mine = jnp.where(jnp.logical_and(low >= 16, low < 16 + HEADS), tile[:8], 0.0)
        rows[k // 4].append(pltpu.roll(mine, H - 16 if k < 4 else H, 1))
    tail = steps + jnp.concatenate(rows[0], axis=0) + jnp.concatenate(rows[1], axis=0)
    tail = tail.astype(BF16)
    for s in range(SEQ):
        send_ref[s, :, : 2 * N] = d_bc
        send_ref[s, :, 2 * N :] = tail


def hidden_kernel(d_ref, wbc_ref, wdt_ref, gh_ref):
    d_bc = d_ref[0, :, : 2 * N]
    d_step = d_ref[0, :, 2 * N :][:, :H]
    gh = dot(d_bc, wbc_ref[...], 1, 1) + dot(d_step, wdt_ref[...])
    gh_ref[...] = gh.astype(BF16)


def finish_kernel(*refs):
    blocks, (y_hbm, gx_hbm), sems = refs[:HEAD], refs[HEAD : HEAD + 2], refs[HEAD + 2]
    copies = []
    for k in range(HEAD):
        of = lax.rem(lax.axis_index("head") + HEAD - k, HEAD)
        cols = pl.ds(pl.multiple_of(of * CH, LANES), CH)
        for i, out in enumerate((y_hbm, gx_hbm)):
            copies.append(
                pltpu.make_async_copy(
                    blocks[k].at[:, i * CH : (i + 1) * CH], out.at[:, cols], sems.at[k, i]
                )
            )
    for copy in copies:
        copy.start()
    for copy in copies:
        copy.wait()


def weight_kernel(d_ref, h_ref, send_ref, par_ref):
    half = TOKENS // 2
    d = d_ref[...]
    h = h_ref[:, :, CH:].astype(F32)
    grad = jnp.zeros((COLS, DPACK), F32)
    for i in range(2):
        rows = h[:, :, i * COLS : (i + 1) * COLS].reshape(SEQ * half, COLS).astype(BF16)
        grad += dot(rows, d[:, i * half : (i + 1) * half].reshape(SEQ * half, DPACK), 0, 0)
    grad = grad.astype(BF16)
    for k in range(HEAD):
        send_ref[k] = grad
    tail = jnp.sum(d[:, :, 2 * N :].astype(F32), axis=0)
    low = iota((8, LANES), 1)
    out = jnp.zeros((8, LANES), F32)
    for k in range(HEAD):
        at = H if k < 4 else H + 16
        rolled = pltpu.roll(tail[8 * (k % 4) : 8 * (k % 4) + 8], (HEADS * k - at) % LANES, 1)
        mine = jnp.logical_and(low >= HEADS * k, low < HEADS * (k + 1))
        out += jnp.where(mine, rolled, 0.0)
    par_ref[...] = ((out[0:3] + out[3:6]) / TOTAL)[:, :H]


def sum_kernel(r_ref, send_ref):
    grad = (jnp.sum(r_ref[...].astype(F32), axis=0) / TOTAL).astype(BF16)
    for s in range(SEQ):
        send_ref[s] = grad


def unpack_kernel(r_ref, bc_hbm, dt_hbm, bc_ref, dt_ref, sems):
    parts = SEQ // STAGES
    copies = []
    for i in range(STAGES):
        part = r_ref[i * parts : (i + 1) * parts]
        at = slice(i * parts * COLS, (i + 1) * parts * COLS)
        bc_ref[at] = part[:, :, : 2 * N].astype(F32).reshape(parts * COLS, 2 * N)
        copies.append(pltpu.make_async_copy(bc_ref.at[at], bc_hbm.at[at], sems.at[i, 0]))
        copies[-1].start()
        dt_ref[:, at] = part[:, :, 2 * N :].astype(F32).reshape(parts * COLS, LANES).T[:H]
        copies.append(pltpu.make_async_copy(dt_ref.at[:, at], dt_hbm.at[:, at], sems.at[i, 1]))
        copies[-1].start()
    for copy in copies:
        copy.wait()


def call(kernel, outs, *args, scratch=(), far=False, limit=LIMIT):
    return pl.pallas_call(
        kernel,
        out_shape=[jax.ShapeDtypeStruct(shape, kind) for shape, kind in outs],
        in_specs=[pl.BlockSpec(memory_space=pltpu.HBM if far else pltpu.VMEM)] * len(args),
        out_specs=[pl.BlockSpec(memory_space=pltpu.VMEM)] * len(outs),
        scratch_shapes=list(scratch),
        compiler_params=pltpu.CompilerParams(vmem_limit_bytes=limit),
    )(*args)


def unpack(w_all):
    return pl.pallas_call(
        unpack_kernel,
        out_shape=[jax.ShapeDtypeStruct((D, 2 * N), F32), jax.ShapeDtypeStruct((H, D), F32)],
        in_specs=[pl.BlockSpec(memory_space=pltpu.VMEM)],
        out_specs=[pl.BlockSpec(memory_space=pltpu.HBM)] * 2,
        scratch_shapes=[
            pltpu.VMEM((D, 2 * N), F32),
            pltpu.VMEM((H, D), F32),
            pltpu.SemaphoreType.DMA((STAGES, 2)),
        ],
        compiler_params=pltpu.CompilerParams(vmem_limit_bytes=LIMIT),
    )(w_all)


def exchange(v, axis):
    return lax.all_to_all(v, axis, split_axis=0, concat_axis=0, tiled=True)


def per_device(hidden, x_input, grad_out, bc_weight, dt_weight, dt_bias, a_log, d_skip):
    prm = jnp.pad(jnp.stack([dt_bias, a_log, d_skip]), ((0, 5), (0, LANES - H)))
    [packed] = call(
        project_kernel,
        [((HEAD, TOKENS, PACK), BF16)],
        hidden, bc_weight, dt_weight.T, x_input, grad_out,
        scratch=[
            pltpu.VMEM((TOKENS, D), BF16),
            pltpu.VMEM((D, 2 * N), BF16),
            pltpu.VMEM((H, D), BF16),
            pltpu.SemaphoreType.DMA((3 + 2 * HEAD,)),
        ],
        far=True,
        limit=FULL,
    )
    mine = exchange(packed, "head").reshape(SPAN, PACK)
    [hid_send] = call(slab_kernel, [((SEQ, TOKENS // 2, 3 * LANES), BF16)], hidden)
    [sent] = call(
        totals_kernel, [((SEQ, 2 * SLAB, CH + 3 * LANES), BF16)], mine, prm, hid_send
    )
    totals = exchange(sent, "seq")
    [inner] = call(
        inner_kernel,
        [((SPAN, PACK), F32)],
        mine, prm,
        scratch=[pltpu.VMEM((SPAN, SPAN), F32)],
    )
    totals, inner = lax.optimization_barrier((totals, inner))
    [states] = call(prefix_kernel, [((SEQ, 2 * SLAB, CH), BF16)], totals)
    states = exchange(states, "seq")
    d_part, both = call(
        carry_kernel,
        [((HEAD, TOKENS, DPACK), BF16), ((SPAN, 2 * CH), BF16)],
        mine, prm, states, inner,
    )
    d_part = exchange(d_part, "head")
    [d_send] = call(reduce_kernel, [((SEQ, TOKENS, DPACK), BF16)], d_part)
    d_all = exchange(d_send, "seq")
    [grad_hidden] = call(
        hidden_kernel, [((TOKENS, D), BF16)], d_send, bc_weight, dt_weight.T
    )
    d_all, grad_hidden = lax.optimization_barrier((d_all, grad_hidden))
    w_send, param_grads = call(
        weight_kernel, [((HEAD, COLS, DPACK), BF16), ((3, H), F32)], d_all, totals
    )
    w_parts = exchange(w_send, "head")
    [w_sum] = call(sum_kernel, [((SEQ, COLS, DPACK), BF16)], w_parts)
    w_sum, both = lax.optimization_barrier((w_sum, both))
    w_all = exchange(w_sum, "seq")
    blocks = list(call(rotate_kernel, [((TOKENS, 2 * CH), BF16)] * HEAD, both))
    for k in range(1, HEAD):
        ring = [(i, (i + k) % HEAD) for i in range(HEAD)]
        blocks[k] = lax.ppermute(blocks[k], "head", ring)
    mixer_out, grad_x = pl.pallas_call(
        finish_kernel,
        out_shape=[jax.ShapeDtypeStruct((TOKENS, H * WIDTH), BF16)] * 2,
        in_specs=[pl.BlockSpec(memory_space=pl.ANY)] * HEAD,
        out_specs=[pl.BlockSpec(memory_space=pltpu.HBM)] * 2,
        scratch_shapes=[pltpu.SemaphoreType.DMA((HEAD, 2))],
        compiler_params=pltpu.CompilerParams(vmem_limit_bytes=LIMIT),
    )(*blocks)
    grad_bc_weight, grad_dt_weight = unpack(w_all)
    return (mixer_out, grad_x, grad_hidden, grad_bc_weight, grad_dt_weight.T, param_grads)


def solution(mesh):
    rows = P(("dp", "seq", "head"), None)
    return jax.shard_map(
        per_device,
        mesh=mesh,
        in_specs=(rows, rows, rows, P(), P(), P(), P(), P()),
        out_specs=(rows, rows, rows, P("dp", None), P("dp", None), P("dp", None)),
        check_vma=False,
    )
```

```python
import functools

import jax
import jax.numpy as jnp
from jax import lax
from jax.experimental import pallas as pl
from jax.experimental.pallas import tpu as pltpu
from jax.sharding import PartitionSpec as P

F32 = jnp.float32
BF16 = jnp.bfloat16
LANES = 128
LIMIT = 24 * 2**20
FULL = 60 * 2**20

SEQ, HEAD = 16, 8
D, H, WIDTH, N = 2560, 80, 64, 128
TOKENS = 32
SPAN = TOKENS * HEAD
HEADS = H // HEAD
CH = HEADS * WIDTH
TOTAL = SPAN * SEQ
COLS = D // SEQ
PACK = 2 * CH + 2 * N + LANES
DPACK = 2 * N + LANES
STAGES = 4
SLAB = N // SEQ
STEP = 2 * CH + 2 * N


def dot(a, b, ca=1, cb=0):
    return lax.dot_general(a, b, (((ca,), (cb,)), ((), ())), preferred_element_type=F32)


def iota(shape, dim):
    return lax.broadcasted_iota(jnp.int32, shape, dim)


def split(v, parts):
    out = []
    for _ in range(parts):
        top = v.astype(BF16)
        out.append(top)
        v = v - top.astype(F32)
    return out


def one_hot(shift=0):
    return (iota((LANES, CH), 0) - shift == iota((LANES, CH), 1) // WIDTH).astype(F32).astype(BF16)


def spread(v, hot):
    hi, lo = split(v, 2)
    return dot(hi, hot) + dot(lo, hot)


def gather_heads(v, hot, parts=2):
    return sum(dot(part, hot, 1, 1) for part in split(v, parts))


def triangle(dim):
    return (iota((SPAN, SPAN), dim) >= iota((SPAN, SPAN), 1 - dim)).astype(F32).astype(BF16)


def running_sum(tri, v):
    return sum(dot(tri, part) for part in split(v, 3))


def head_params(prm_ref):
    prm = pltpu.roll(prm_ref[...], lax.rem(LANES - HEADS * lax.axis_index("head"), LANES), 1)
    return prm[0:1], -jnp.exp(prm[1:2]), prm[2:3]


def step_sizes(r_ref, prm_ref):
    bias, rate, skip = head_params(prm_ref)
    pre = r_ref[:, STEP:].astype(F32) + bias
    step = jnp.maximum(pre, 0.0) + jnp.log1p(jnp.exp(-jnp.abs(pre)))
    cum = running_sum(triangle(0), step * rate)
    return pre, step, cum, rate, skip


def project_kernel(
    hid_hbm, wbc_hbm, wdt_hbm, x_hbm, g_hbm, send_hbm, tail_ref, x_ref, g_ref, hid_ref, wbc_ref, wdt_ref, sems
):
    rows = D // STAGES
    chunks = [slice(i * rows, (i + 1) * rows) for i in range(STAGES)]
    first = [
        pltpu.make_async_copy(hid_hbm, hid_ref, sems.at[0]),
        pltpu.make_async_copy(wdt_hbm, wdt_ref, sems.at[1]),
    ]
    for i, at in enumerate(chunks):
        first.append(pltpu.make_async_copy(wbc_hbm.at[at], wbc_ref.at[at], sems.at[2 + i]))
    given = []
    for i, (far, near) in enumerate(((x_hbm, x_ref), (g_hbm, g_ref))):
        given.append(pltpu.make_async_copy(far, near, sems.at[2 + STAGES + i]))
    for copy in first + given:
        copy.start()
    rest = []
    for i, near in enumerate((x_ref, g_ref)):
        given[i].wait()
        for k in range(HEAD):
            rest.append(
                pltpu.make_async_copy(
                    near.at[:, k * CH : (k + 1) * CH],
                    send_hbm.at[k, :, i * CH : (i + 1) * CH],
                    sems.at[4 + STAGES + 2 * k + i],
                )
            )
            rest[-1].start()
    first[0].wait()
    first[1].wait()
    raw = dot(hid_ref[...], wdt_ref[...], 1, 1).astype(BF16).astype(F32)
    raw = jnp.concatenate([raw, jnp.zeros((TOKENS, LANES - H), F32)], axis=1)
    lane = iota((TOKENS, LANES), 1)
    for k in range(HEAD):
        mine = pltpu.roll(raw, (LANES - HEADS * k) % LANES, 1)
        tail_ref[k, :, 2 * N :] = jnp.where(lane < HEADS, mine, 0.0).astype(BF16)
    bc = jnp.zeros((TOKENS, 2 * N), F32)
    for i, at in enumerate(chunks):
        first[2 + i].wait()
        bc += dot(hid_ref[:, at], wbc_ref[at])
    for k in range(HEAD):
        tail_ref[k, :, : 2 * N] = bc.astype(BF16)
    last = pltpu.make_async_copy(
        tail_ref, send_hbm.at[:, :, 2 * CH :], sems.at[4 + STAGES + 2 * HEAD]
    )
    last.start()
    for copy in rest:
        copy.wait()
    last.wait()


def slab_kernel(hid_ref, hs_ref):
    half = TOKENS // 2
    wide = hid_ref[...].astype(F32)
    pad = jnp.zeros((half, 3 * LANES - 2 * COLS), F32)
    for s in range(SEQ):
        part = wide[:, s * COLS : (s + 1) * COLS]
        hs_ref[s] = jnp.concatenate([part[:half], part[half:], pad], axis=1).astype(BF16)


def totals_kernel(r_ref, prm_ref, hs_ref, send_ref):
    pre, step, cum, rate, skip = step_sizes(r_ref, prm_ref)
    hot = one_hot()
    total = cum[SPAN - 1 :]
    to_end = spread(step * jnp.exp(total - cum), hot)
    from_start = spread(jnp.exp(cum), hot)
    x = r_ref[:, :CH].astype(F32)
    g = r_ref[:, CH : 2 * CH].astype(F32)
    b = r_ref[:, 2 * CH : 2 * CH + N]
    c = r_ref[:, 2 * CH + N : STEP]
    fresh = dot(b, (x * to_end).astype(BF16), 0, 0)
    back = dot(c, (g * from_start).astype(BF16), 0, 0)
    both = jnp.concatenate(
        [fresh.reshape(SEQ, SLAB, CH), back.reshape(SEQ, SLAB, CH)], axis=1
    )
    send_ref[:, :, :CH] = both.astype(BF16)
    hi, lo = split(jnp.exp(total), 2)
    row = iota((2 * SLAB, LANES), 0)
    lane = iota((2 * SLAB, LANES), 1)
    decay = jnp.where(row == 0, hi.astype(F32), jnp.where(row == 1, lo.astype(F32), 0.0))
    decay = pltpu.roll(jnp.where(lane < HEADS, decay, 0.0), WIDTH, 1)
    send_ref[:, :, CH : CH + 2 * LANES] = hs_ref[:, :, : 2 * LANES]
    tail = hs_ref[:, :, 2 * LANES :].astype(F32) + decay[None]
    send_ref[:, :, CH + 2 * LANES :] = tail.astype(BF16)


def prefix_kernel(r_ref, out_ref):
    hot = one_hot(WIDTH)
    tail = r_ref[:, :, CH + 2 * LANES :].astype(F32)
    decay = dot(tail[:, 0, :].astype(BF16), hot) + dot(tail[:, 1, :].astype(BF16), hot)
    ahead, behind = [], [None] * SEQ
    state = jnp.zeros((SLAB, CH), F32)
    for s in range(SEQ):
        ahead.append(state)
        state = decay[s : s + 1] * state + r_ref[s, :, :CH].astype(F32)[:SLAB]
    state = jnp.zeros((SLAB, CH), F32)
    for s in reversed(range(SEQ)):
        behind[s] = state
        state = decay[s : s + 1] * state + r_ref[s, :, :CH].astype(F32)[SLAB:]
    for s in range(SEQ):
        out_ref[s] = jnp.concatenate([ahead[s], behind[s]], axis=0).astype(BF16)


def inner_kernel(r_ref, prm_ref, out_ref, ds_ref):
    pre, step, cum, rate, skip = step_sizes(r_ref, prm_ref)
    hot = one_hot()
    cum_t = cum.T
    b = r_ref[:, 2 * CH : 2 * CH + N]
    c = r_ref[:, 2 * CH + N : STEP]
    scores = dot(c, b, 1, 1)
    causal = iota((SPAN, SPAN), 0) >= iota((SPAN, SPAN), 1)
    step_x = spread(step, hot)
    low = iota((SPAN, LANES), 1) < WIDTH
    zero = jnp.zeros((SPAN, LANES), BF16)
    products = []
    for j in range(HEADS // 2):
        at = slice(j * LANES, (j + 1) * LANES)
        g = r_ref[:, CH + j * LANES : CH + (j + 1) * LANES]
        u = (r_ref[:, at].astype(F32) * step_x[:, at]).astype(BF16)
        g_t = g.astype(F32).T.astype(BF16)
        y = jnp.zeros((SPAN, LANES), F32)
        du_t = []
        for i in range(2):
            h = 2 * j + i
            mine = low if i == 0 else jnp.logical_not(low)
            gap = jnp.where(causal, cum[:, h : h + 1] - cum_t[h : h + 1, :], -1e30)
            decay = jnp.exp(gap)
            mixer = (decay * scores).astype(BF16)
            y += dot(mixer, jnp.where(mine, u, zero))
            du_t.append(dot(g_t[i * WIDTH : (i + 1) * WIDTH], mixer))
            d_mixer = dot(jnp.where(mine, g, zero), u, 1, 1) * decay
            if h == 0:
                ds_ref[...] = d_mixer
            else:
                ds_ref[...] += d_mixer
        du = jnp.concatenate(du_t, axis=0).T
        out_ref[:, at] = y
        out_ref[:, CH + j * LANES : CH + (j + 1) * LANES] = du
        products.append(g.astype(F32) * y - u.astype(F32) * du)
    out_ref[:, STEP:] = gather_heads(jnp.concatenate(products, axis=1), hot, 3)
    ds = ds_ref[...]
    out_ref[:, 2 * CH : 2 * CH + N] = dot(ds.T.astype(BF16), c)
    out_ref[:, 2 * CH + N : STEP] = dot(ds.astype(BF16), b)


def carry_kernel(r_ref, prm_ref, st_ref, in_ref, send_ref, both_ref):
    pre, step, cum, rate, skip = step_sizes(r_ref, prm_ref)
    hot = one_hot()
    total = cum[SPAN - 1 :]
    step_x = spread(step, hot)
    to_end = spread(jnp.exp(total - cum), hot)
    from_start = spread(jnp.exp(cum), hot)
    skip_x = spread(jnp.broadcast_to(skip, (8, LANES)), hot)[:1]
    states = st_ref[...].astype(F32)
    state_in = states[:, :SLAB].reshape(N, CH)
    state_gr = states[:, SLAB:].reshape(N, CH)
    x = r_ref[:, :CH].astype(F32)
    g = r_ref[:, CH : 2 * CH].astype(F32)
    b = r_ref[:, 2 * CH : 2 * CH + N]
    c = r_ref[:, 2 * CH + N : STEP]
    s_b = state_in.astype(BF16)
    q_b = state_gr.astype(BF16)
    u = x * step_x
    carried = dot(c, s_b) * from_start
    late = dot(b, q_b) * to_end
    y = in_ref[:, :CH] + carried + skip_x * x
    du = in_ref[:, CH : 2 * CH] + late
    gx = step_x * du + skip_x * g
    d_c = in_ref[:, 2 * CH + N : STEP] + dot((g * from_start).astype(BF16), s_b, 1, 1)
    d_b = in_ref[:, 2 * CH : 2 * CH + N] + dot((u * to_end).astype(BF16), q_b, 1, 1)
    e = in_ref[:, STEP:] + gather_heads(g * carried, hot)
    f = gather_heads(u * late, hot)
    xdu = gather_heads(x * du, hot)
    sums = jnp.concatenate(
        [
            jnp.sum(state_in * state_gr, axis=0, keepdims=True),
            jnp.sum(g * x, axis=0, keepdims=True),
            jnp.zeros((6, CH), F32),
        ],
        axis=0,
    )
    sums = gather_heads(sums, hot, 3)
    edge = jnp.exp(total) * sums[0:1]
    d_rate = running_sum(triangle(1), e) + running_sum(triangle(0), f) - f + edge
    d_raw = (rate * d_rate + xdu) / (1.0 + jnp.exp(-pre))
    d_bias = jnp.sum(d_raw, axis=0, keepdims=True)
    d_log = rate * jnp.sum(step * d_rate, axis=0, keepdims=True)
    hi, lo = split(jnp.concatenate([d_bias, d_log, sums[1:2]], axis=0), 2)
    row = jnp.concatenate(
        [hi.astype(F32), lo.astype(F32), jnp.zeros((TOKENS - 6, LANES), F32)], axis=0
    )
    lane = iota((TOKENS, LANES), 1)
    row = pltpu.roll(jnp.where(lane < HEADS, row, 0.0), 16, 1)
    both_ref[:, :CH] = y.astype(BF16)
    both_ref[:, CH:] = gx.astype(BF16)
    for k in range(HEAD):
        at = slice(k * TOKENS, (k + 1) * TOKENS)
        send_ref[k, :, :N] = d_b[at].astype(BF16)
        send_ref[k, :, N : 2 * N] = d_c[at].astype(BF16)
        send_ref[k, :, 2 * N :] = (jnp.where(lane < HEADS, d_raw[at], 0.0) + row).astype(BF16)


def rotate_kernel(both_ref, *blocks):
    for k in range(HEAD):
        to = lax.rem(lax.axis_index("head") + k, HEAD)
        blocks[k][...] = both_ref[pl.ds(pl.multiple_of(to * TOKENS, TOKENS), TOKENS), :]


def reduce_kernel(r_ref, send_ref):
    d_bc = jnp.sum(r_ref[:, :, : 2 * N].astype(F32), axis=0).astype(BF16)
    lane = iota((TOKENS, LANES), 1)
    steps = jnp.zeros((TOKENS, LANES), F32)
    rows = [[], []]
    low = iota((8, LANES), 1)
    for k in range(HEAD):
        tile = r_ref[k, :, 2 * N :].astype(F32)
        steps += pltpu.roll(jnp.where(lane < HEADS, tile, 0.0), HEADS * k, 1)
        mine = jnp.where(jnp.logical_and(low >= 16, low < 16 + HEADS), tile[:8], 0.0)
        rows[k // 4].append(pltpu.roll(mine, H - 16 if k < 4 else H, 1))
    tail = steps + jnp.concatenate(rows[0], axis=0) + jnp.concatenate(rows[1], axis=0)
    tail = tail.astype(BF16)
    for s in range(SEQ):
        send_ref[s, :, : 2 * N] = d_bc
        send_ref[s, :, 2 * N :] = tail


def hidden_kernel(d_ref, wbc_ref, wdt_ref, gh_ref):
    d_bc = d_ref[0, :, : 2 * N]
    d_step = d_ref[0, :, 2 * N :][:, :H]
    gh = dot(d_bc, wbc_ref[...], 1, 1) + dot(d_step, wdt_ref[...])
    gh_ref[...] = gh.astype(BF16)


def finish_kernel(*refs):
    blocks, (y_hbm, gx_hbm), sems = refs[:HEAD], refs[HEAD : HEAD + 2], refs[HEAD + 2]
    copies = []
    for k in range(HEAD):
        of = lax.rem(lax.axis_index("head") + HEAD - k, HEAD)
        cols = pl.ds(pl.multiple_of(of * CH, LANES), CH)
        for i, out in enumerate((y_hbm, gx_hbm)):
            copies.append(
                pltpu.make_async_copy(
                    blocks[k].at[:, i * CH : (i + 1) * CH], out.at[:, cols], sems.at[k, i]
                )
            )
    for copy in copies:
        copy.start()
    for copy in copies:
        copy.wait()


def weight_kernel(d_ref, h_ref, send_ref, par_ref):
    half = TOKENS // 2
    d = d_ref[...]
    h = h_ref[:, :, CH:].astype(F32)
    grad = jnp.zeros((COLS, DPACK), F32)
    for i in range(2):
        rows = h[:, :, i * COLS : (i + 1) * COLS].reshape(SEQ * half, COLS).astype(BF16)
        grad += dot(rows, d[:, i * half : (i + 1) * half].reshape(SEQ * half, DPACK), 0, 0)
    send_ref[...] = (grad / TOTAL).astype(BF16)
    tail = jnp.sum(d[:, :, 2 * N :].astype(F32), axis=0)
    low = iota((8, LANES), 1)
    out = jnp.zeros((8, LANES), F32)
    for k in range(HEAD):
        at = H if k < 4 else H + 16
        rolled = pltpu.roll(tail[8 * (k % 4) : 8 * (k % 4) + 8], (HEADS * k - at) % LANES, 1)
        mine = jnp.logical_and(low >= HEADS * k, low < HEADS * (k + 1))
        out += jnp.where(mine, rolled, 0.0)
    par_ref[...] = ((out[0:3] + out[3:6]) / TOTAL)[:, :H]


def add_kernel(a_ref, b_ref, out_ref):
    out_ref[...] = (a_ref[...].astype(F32) + b_ref[...].astype(F32)).astype(BF16)


def spread_kernel(a_ref, b_ref, send_ref):
    total = (a_ref[...].astype(F32) + b_ref[...].astype(F32)).astype(BF16)
    for s in range(SEQ):
        send_ref[s] = total


def unpack_kernel(r_ref, bc_hbm, dt_hbm, bc_ref, dt_ref, sems):
    parts = SEQ // STAGES
    copies = []
    for i in range(STAGES):
        part = r_ref[i * parts : (i + 1) * parts]
        at = slice(i * parts * COLS, (i + 1) * parts * COLS)
        bc_ref[at] = part[:, :, : 2 * N].astype(F32).reshape(parts * COLS, 2 * N)
        copies.append(pltpu.make_async_copy(bc_ref.at[at], bc_hbm.at[at], sems.at[i, 0]))
        copies[-1].start()
        dt_ref[:, at] = part[:, :, 2 * N :].astype(F32).reshape(parts * COLS, LANES).T[:H]
        copies.append(pltpu.make_async_copy(dt_ref.at[:, at], dt_hbm.at[:, at], sems.at[i, 1]))
        copies[-1].start()
    for copy in copies:
        copy.wait()


def call(kernel, outs, *args, scratch=(), far=False, far_out=False, limit=LIMIT):
    return pl.pallas_call(
        kernel,
        out_shape=[jax.ShapeDtypeStruct(shape, kind) for shape, kind in outs],
        in_specs=[pl.BlockSpec(memory_space=pltpu.HBM if far else pltpu.VMEM)] * len(args),
        out_specs=[pl.BlockSpec(memory_space=pltpu.HBM if far_out else pltpu.VMEM)] * len(outs),
        scratch_shapes=list(scratch),
        compiler_params=pltpu.CompilerParams(vmem_limit_bytes=limit),
    )(*args)


def unpack(w_all):
    return pl.pallas_call(
        unpack_kernel,
        out_shape=[jax.ShapeDtypeStruct((D, 2 * N), F32), jax.ShapeDtypeStruct((H, D), F32)],
        in_specs=[pl.BlockSpec(memory_space=pltpu.VMEM)],
        out_specs=[pl.BlockSpec(memory_space=pltpu.HBM)] * 2,
        scratch_shapes=[
            pltpu.VMEM((D, 2 * N), F32),
            pltpu.VMEM((H, D), F32),
            pltpu.SemaphoreType.DMA((STAGES, 2)),
        ],
        compiler_params=pltpu.CompilerParams(vmem_limit_bytes=LIMIT),
    )(w_all)


def exchange(v, axis):
    return lax.all_to_all(v, axis, split_axis=0, concat_axis=0, tiled=True)


def per_device(hidden, x_input, grad_out, bc_weight, dt_weight, dt_bias, a_log, d_skip):
    prm = jnp.pad(jnp.stack([dt_bias, a_log, d_skip]), ((0, 5), (0, LANES - H)))
    [packed] = call(
        project_kernel,
        [((HEAD, TOKENS, PACK), BF16)],
        hidden, bc_weight, dt_weight.T, x_input, grad_out,
        scratch=[
            pltpu.VMEM((HEAD, TOKENS, DPACK), BF16),
            pltpu.VMEM((TOKENS, H * WIDTH), BF16),
            pltpu.VMEM((TOKENS, H * WIDTH), BF16),
            pltpu.VMEM((TOKENS, D), BF16),
            pltpu.VMEM((D, 2 * N), BF16),
            pltpu.VMEM((H, D), BF16),
            pltpu.SemaphoreType.DMA((5 + STAGES + 2 * HEAD,)),
        ],
        far=True,
        far_out=True,
        limit=FULL,
    )
    mine = exchange(packed, "head").reshape(SPAN, PACK)
    [hid_send] = call(slab_kernel, [((SEQ, TOKENS // 2, 3 * LANES), BF16)], hidden)
    [sent] = call(
        totals_kernel, [((SEQ, 2 * SLAB, CH + 3 * LANES), BF16)], mine, prm, hid_send
    )
    totals = exchange(sent, "seq")
    [inner] = call(
        inner_kernel,
        [((SPAN, PACK), F32)],
        mine, prm,
        scratch=[pltpu.VMEM((SPAN, SPAN), F32)],
    )
    totals, inner = lax.optimization_barrier((totals, inner))
    [states] = call(prefix_kernel, [((SEQ, 2 * SLAB, CH), BF16)], totals)
    states = exchange(states, "seq")
    d_part, both = call(
        carry_kernel,
        [((HEAD, TOKENS, DPACK), BF16), ((SPAN, 2 * CH), BF16)],
        mine, prm, states, inner,
    )
    d_part = exchange(d_part, "head")
    [d_send] = call(
        reduce_kernel,
        [((SEQ, TOKENS, DPACK), BF16)],
        d_part,
    )
    d_all = exchange(d_send, "seq")
    [grad_hidden] = call(
        hidden_kernel, [((TOKENS, D), BF16)], d_send, bc_weight, dt_weight.T
    )
    d_all, grad_hidden = lax.optimization_barrier((d_all, grad_hidden))
    w_part, param_grads = call(
        weight_kernel, [((COLS, DPACK), BF16), ((3, H), F32)], d_all, totals
    )
    for far in (1, 2):
        other = lax.ppermute(w_part, "head", [(i, i ^ far) for i in range(HEAD)])
        [w_part] = call(add_kernel, [((COLS, DPACK), BF16)], w_part, other)
    other = lax.ppermute(w_part, "head", [(i, i ^ 4) for i in range(HEAD)])
    [w_sum] = call(
        spread_kernel,
        [((SEQ, COLS, DPACK), BF16)],
        w_part, other,
    )
    w_sum, both = lax.optimization_barrier((w_sum, both))
    w_all = exchange(w_sum, "seq")
    blocks = list(call(rotate_kernel, [((TOKENS, 2 * CH), BF16)] * HEAD, both))
    for k in range(1, HEAD):
        ring = [(i, (i + k) % HEAD) for i in range(HEAD)]
        blocks[k] = lax.ppermute(blocks[k], "head", ring)
    mixer_out, grad_x = pl.pallas_call(
        finish_kernel,
        out_shape=[jax.ShapeDtypeStruct((TOKENS, H * WIDTH), BF16)] * 2,
        in_specs=[pl.BlockSpec(memory_space=pl.ANY)] * HEAD,
        out_specs=[pl.BlockSpec(memory_space=pltpu.HBM)] * 2,
        scratch_shapes=[pltpu.SemaphoreType.DMA((HEAD, 2))],
        compiler_params=pltpu.CompilerParams(vmem_limit_bytes=LIMIT),
    )(*blocks)
    grad_bc_weight, grad_dt_weight = unpack(w_all)
    return (mixer_out, grad_x, grad_hidden, grad_bc_weight, grad_dt_weight.T, param_grads)


def solution(mesh):
    rows = P(("dp", "seq", "head"), None)
    return jax.shard_map(
        per_device,
        mesh=mesh,
        in_specs=(rows, rows, rows, P(), P(), P(), P(), P()),
        out_specs=(rows, rows, rows, P("dp", None), P("dp", None), P("dp", None)),
        check_vma=False,
    )
```

```python
import functools

import jax
import jax.numpy as jnp
from jax import lax
from jax.experimental import pallas as pl
from jax.experimental.pallas import tpu as pltpu
from jax.sharding import PartitionSpec as P

F32 = jnp.float32
BF16 = jnp.bfloat16
LANES = 128
LIMIT = 24 * 2**20
NEAR = 52 * 2**20
FULL = 60 * 2**20

SEQ, HEAD = 16, 8
D, H, WIDTH, N = 2560, 80, 64, 128
TOKENS = 32
SPAN = TOKENS * HEAD
HEADS = H // HEAD
CH = HEADS * WIDTH
TOTAL = SPAN * SEQ
COLS = D // SEQ
PACK = 2 * CH + 2 * N + LANES
DPACK = 2 * N + LANES
STAGES = 4
SLAB = N // SEQ
STEP = 2 * CH + 2 * N


def dot(a, b, ca=1, cb=0):
    return lax.dot_general(a, b, (((ca,), (cb,)), ((), ())), preferred_element_type=F32)


def iota(shape, dim):
    return lax.broadcasted_iota(jnp.int32, shape, dim)


def split(v, parts):
    out = []
    for _ in range(parts):
        top = v.astype(BF16)
        out.append(top)
        v = v - top.astype(F32)
    return out


def one_hot(shift=0):
    return (iota((LANES, CH), 0) - shift == iota((LANES, CH), 1) // WIDTH).astype(F32).astype(BF16)


def spread(v, hot):
    hi, lo = split(v, 2)
    return dot(hi, hot) + dot(lo, hot)


def gather_heads(v, hot, parts=2):
    return sum(dot(part, hot, 1, 1) for part in split(v, parts))


def triangle(dim):
    return (iota((SPAN, SPAN), dim) >= iota((SPAN, SPAN), 1 - dim)).astype(F32).astype(BF16)


def running_sum(tri, v):
    return sum(dot(tri, part) for part in split(v, 3))


def head_params(prm_ref):
    prm = pltpu.roll(prm_ref[...], lax.rem(LANES - HEADS * lax.axis_index("head"), LANES), 1)
    return prm[0:1], -jnp.exp(prm[1:2]), prm[2:3]


def step_sizes(r_ref, prm_ref, cum=None):
    bias, rate, skip = head_params(prm_ref)
    pre = r_ref[:, STEP:].astype(F32) + bias
    step = jnp.maximum(pre, 0.0) + jnp.log1p(jnp.exp(-jnp.abs(pre)))
    if cum is None:
        cum = running_sum(triangle(0), step * rate)
    return pre, step, cum, rate, skip


def project_kernel(
    hid_hbm, wbc_hbm, wdt_hbm, x_hbm, g_hbm, send_hbm, pack_ref, x_ref, g_ref, hid_ref, wbc_ref, wdt_ref, sems
):
    half = D // 2
    halves = [slice(0, half), slice(half, D)]
    come = [
        pltpu.make_async_copy(far, near, sems.at[i])
        for i, (far, near) in enumerate(
            [(x_hbm, x_ref), (g_hbm, g_ref), (hid_hbm, hid_ref), (wdt_hbm, wdt_ref)]
            + [(wbc_hbm.at[at], wbc_ref.at[at]) for at in halves]
        )
    ]
    go = [
        pltpu.make_async_copy(pack_ref.at[:, :, at], send_hbm.at[:, :, at], sems.at[len(come) + i])
        for i, at in enumerate((slice(0, 2 * CH), slice(2 * CH, PACK)))
    ]
    for copy in come:
        copy.start()
    for i, ref in enumerate((x_ref, g_ref)):
        come[i].wait()
        for k in range(HEAD):
            pack_ref[k, :, i * CH : (i + 1) * CH] = ref[:, k * CH : (k + 1) * CH]
    go[0].start()
    come[2].wait()
    come[3].wait()
    raw = dot(hid_ref[...], wdt_ref[...], 1, 1).astype(BF16).astype(F32)
    raw = jnp.concatenate([raw, jnp.zeros((TOKENS, LANES - H), F32)], axis=1)
    lane = iota((TOKENS, LANES), 1)
    for k in range(HEAD):
        mine = pltpu.roll(raw, (LANES - HEADS * k) % LANES, 1)
        pack_ref[k, :, STEP:] = jnp.where(lane < HEADS, mine, 0.0).astype(BF16)
    bc = jnp.zeros((TOKENS, 2 * N), F32)
    for i, at in enumerate(halves):
        come[4 + i].wait()
        bc += dot(hid_ref[:, at], wbc_ref[at])
    for k in range(HEAD):
        pack_ref[k, :, 2 * CH : STEP] = bc.astype(BF16)
    go[1].start()
    for copy in go:
        copy.wait()


def slab_kernel(hid_ref, hs_ref):
    half = TOKENS // 2
    wide = hid_ref[...].astype(F32)
    pad = jnp.zeros((half, 3 * LANES - 2 * COLS), F32)
    for s in range(SEQ):
        part = wide[:, s * COLS : (s + 1) * COLS]
        hs_ref[s] = jnp.concatenate([part[:half], part[half:], pad], axis=1).astype(BF16)


def totals_kernel(r_ref, prm_ref, hs_ref, send_ref):
    pre, step, cum, rate, skip = step_sizes(r_ref, prm_ref)
    hot = one_hot()
    total = cum[SPAN - 1 :]
    to_end = spread(step * jnp.exp(total - cum), hot)
    from_start = spread(jnp.exp(cum), hot)
    x = r_ref[:, :CH].astype(F32)
    g = r_ref[:, CH : 2 * CH].astype(F32)
    b = r_ref[:, 2 * CH : 2 * CH + N]
    c = r_ref[:, 2 * CH + N : STEP]
    fresh = dot(b, (x * to_end).astype(BF16), 0, 0)
    back = dot(c, (g * from_start).astype(BF16), 0, 0)
    both = jnp.concatenate(
        [fresh.reshape(SEQ, SLAB, CH), back.reshape(SEQ, SLAB, CH)], axis=1
    )
    send_ref[:, :, :CH] = both.astype(BF16)
    hi, lo = split(jnp.exp(total), 2)
    row = iota((2 * SLAB, LANES), 0)
    lane = iota((2 * SLAB, LANES), 1)
    decay = jnp.where(row == 0, hi.astype(F32), jnp.where(row == 1, lo.astype(F32), 0.0))
    decay = pltpu.roll(jnp.where(lane < HEADS, decay, 0.0), WIDTH, 1)
    send_ref[:, :, CH : CH + 2 * LANES] = hs_ref[:, :, : 2 * LANES]
    tail = hs_ref[:, :, 2 * LANES :].astype(F32) + decay[None]
    send_ref[:, :, CH + 2 * LANES :] = tail.astype(BF16)


def prefix_kernel(r_ref, out_ref):
    hot = one_hot(WIDTH)
    tail = r_ref[:, :, CH + 2 * LANES :].astype(F32)
    decay = dot(tail[:, 0, :].astype(BF16), hot) + dot(tail[:, 1, :].astype(BF16), hot)
    ahead, behind = [], [None] * SEQ
    state = jnp.zeros((SLAB, CH), F32)
    for s in range(SEQ):
        ahead.append(state)
        state = decay[s : s + 1] * state + r_ref[s, :, :CH].astype(F32)[:SLAB]
    state = jnp.zeros((SLAB, CH), F32)
    for s in reversed(range(SEQ)):
        behind[s] = state
        state = decay[s : s + 1] * state + r_ref[s, :, :CH].astype(F32)[SLAB:]
    for s in range(SEQ):
        out_ref[s] = jnp.concatenate([ahead[s], behind[s]], axis=0).astype(BF16)


def inner_kernel(r_ref, prm_ref, out_ref, ds_ref):
    pre, step, cum, rate, skip = step_sizes(r_ref, prm_ref)
    hot = one_hot()
    cum_t = cum.T
    b = r_ref[:, 2 * CH : 2 * CH + N]
    c = r_ref[:, 2 * CH + N : STEP]
    scores = dot(c, b, 1, 1)
    causal = iota((SPAN, SPAN), 0) >= iota((SPAN, SPAN), 1)
    step_x = spread(step, hot)
    low = iota((SPAN, LANES), 1) < WIDTH
    zero = jnp.zeros((SPAN, LANES), BF16)
    products = []
    for j in range(HEADS // 2):
        at = slice(j * LANES, (j + 1) * LANES)
        g = r_ref[:, CH + j * LANES : CH + (j + 1) * LANES]
        u = (r_ref[:, at].astype(F32) * step_x[:, at]).astype(BF16)
        g_t = g.astype(F32).T.astype(BF16)
        y = jnp.zeros((SPAN, LANES), F32)
        du_t = []
        for i in range(2):
            h = 2 * j + i
            mine = low if i == 0 else jnp.logical_not(low)
            gap = jnp.where(causal, cum[:, h : h + 1] - cum_t[h : h + 1, :], -1e30)
            decay = jnp.exp(gap)
            mixer = (decay * scores).astype(BF16)
            y += dot(mixer, jnp.where(mine, u, zero))
            du_t.append(dot(g_t[i * WIDTH : (i + 1) * WIDTH], mixer))
            d_mixer = dot(jnp.where(mine, g, zero), u, 1, 1) * decay
            if h == 0:
                ds_ref[...] = d_mixer
            else:
                ds_ref[...] += d_mixer
        du = jnp.concatenate(du_t, axis=0).T
        out_ref[:, at] = y
        out_ref[:, CH + j * LANES : CH + (j + 1) * LANES] = du
        products.append(g.astype(F32) * y - u.astype(F32) * du)
    out_ref[:, PACK:] = cum
    out_ref[:, STEP:PACK] = gather_heads(jnp.concatenate(products, axis=1), hot, 3)
    ds = ds_ref[...]
    out_ref[:, 2 * CH : 2 * CH + N] = dot(ds.T.astype(BF16), c)
    out_ref[:, 2 * CH + N : STEP] = dot(ds.astype(BF16), b)


def carry_kernel(r_ref, prm_ref, st_ref, in_ref, send_ref, both_ref):
    pre, step, cum, rate, skip = step_sizes(r_ref, prm_ref, in_ref[:, PACK:])
    hot = one_hot()
    total = cum[SPAN - 1 :]
    step_x = spread(step, hot)
    to_end = spread(jnp.exp(total - cum), hot)
    from_start = spread(jnp.exp(cum), hot)
    skip_x = spread(jnp.broadcast_to(skip, (8, LANES)), hot)[:1]
    states = st_ref[...].astype(F32)
    state_in = states[:, :SLAB].reshape(N, CH)
    state_gr = states[:, SLAB:].reshape(N, CH)
    x = r_ref[:, :CH].astype(F32)
    g = r_ref[:, CH : 2 * CH].astype(F32)
    b = r_ref[:, 2 * CH : 2 * CH + N]
    c = r_ref[:, 2 * CH + N : STEP]
    s_b = state_in.astype(BF16)
    q_b = state_gr.astype(BF16)
    u = x * step_x
    carried = dot(c, s_b) * from_start
    late = dot(b, q_b) * to_end
    y = in_ref[:, :CH] + carried + skip_x * x
    du = in_ref[:, CH : 2 * CH] + late
    gx = step_x * du + skip_x * g
    d_c = in_ref[:, 2 * CH + N : STEP] + dot((g * from_start).astype(BF16), s_b, 1, 1)
    d_b = in_ref[:, 2 * CH : 2 * CH + N] + dot((u * to_end).astype(BF16), q_b, 1, 1)
    e = in_ref[:, STEP:PACK] + gather_heads(g * carried, hot)
    f = gather_heads(u * late, hot)
    xdu = gather_heads(x * du, hot)
    sums = jnp.concatenate(
        [
            jnp.sum(state_in * state_gr, axis=0, keepdims=True),
            jnp.sum(g * x, axis=0, keepdims=True),
            jnp.zeros((6, CH), F32),
        ],
        axis=0,
    )
    sums = gather_heads(sums, hot, 3)
    edge = jnp.exp(total) * sums[0:1]
    d_rate = running_sum(triangle(1), e) + running_sum(triangle(0), f) - f + edge
    d_raw = (rate * d_rate + xdu) / (1.0 + jnp.exp(-pre))
    d_bias = jnp.sum(d_raw, axis=0, keepdims=True)
    d_log = rate * jnp.sum(step * d_rate, axis=0, keepdims=True)
    hi, lo = split(jnp.concatenate([d_bias, d_log, sums[1:2]], axis=0), 2)
    row = jnp.concatenate(
        [hi.astype(F32), lo.astype(F32), jnp.zeros((TOKENS - 6, LANES), F32)], axis=0
    )
    lane = iota((TOKENS, LANES), 1)
    row = pltpu.roll(jnp.where(lane < HEADS, row, 0.0), 16, 1)
    both_ref[:, :CH] = y.astype(BF16)
    both_ref[:, CH:] = gx.astype(BF16)
    for k in range(HEAD):
        at = slice(k * TOKENS, (k + 1) * TOKENS)
        send_ref[k, :, :N] = d_b[at].astype(BF16)
        send_ref[k, :, N : 2 * N] = d_c[at].astype(BF16)
        send_ref[k, :, 2 * N :] = (jnp.where(lane < HEADS, d_raw[at], 0.0) + row).astype(BF16)


def rotate_kernel(both_ref, *blocks):
    for k in range(HEAD):
        to = lax.rem(lax.axis_index("head") + k, HEAD)
        blocks[k][...] = both_ref[pl.ds(pl.multiple_of(to * TOKENS, TOKENS), TOKENS), :]


def reduce_kernel(r_ref, send_ref):
    d_bc = jnp.sum(r_ref[:, :, : 2 * N].astype(F32), axis=0).astype(BF16)
    lane = iota((TOKENS, LANES), 1)
    steps = jnp.zeros((TOKENS, LANES), F32)
    rows = [[], []]
    low = iota((8, LANES), 1)
    for k in range(HEAD):
        tile = r_ref[k, :, 2 * N :].astype(F32)
        steps += pltpu.roll(jnp.where(lane < HEADS, tile, 0.0), HEADS * k, 1)
        mine = jnp.where(jnp.logical_and(low >= 16, low < 16 + HEADS), tile[:8], 0.0)
        rows[k // 4].append(pltpu.roll(mine, H - 16 if k < 4 else H, 1))
    tail = steps + jnp.concatenate(rows[0], axis=0) + jnp.concatenate(rows[1], axis=0)
    tail = tail.astype(BF16)
    for s in range(SEQ):
        send_ref[s, :, : 2 * N] = d_bc
        send_ref[s, :, 2 * N :] = tail


def hidden_kernel(d_ref, wbc_ref, wdt_ref, gh_ref):
    d_bc = d_ref[0, :, : 2 * N]
    d_step = d_ref[0, :, 2 * N :][:, :H]
    gh = dot(d_bc, wbc_ref[...], 1, 1) + dot(d_step, wdt_ref[...])
    gh_ref[...] = gh.astype(BF16)


def finish_kernel(*refs):
    blocks, outs = refs[:HEAD], refs[HEAD:]
    for k in range(HEAD):
        of = lax.rem(lax.axis_index("head") + HEAD - k, HEAD)
        cols = pl.ds(pl.multiple_of(of * CH, LANES), CH)
        for i, out_ref in enumerate(outs):
            out_ref[:, cols] = blocks[k][:, i * CH : (i + 1) * CH]


def weight_kernel(d_ref, h_ref, send_ref, par_ref):
    half = TOKENS // 2
    d = d_ref[...]
    h = h_ref[:, :, CH:].astype(F32)
    grad = jnp.zeros((COLS, DPACK), F32)
    for i in range(2):
        rows = h[:, :, i * COLS : (i + 1) * COLS].reshape(SEQ * half, COLS).astype(BF16)
        grad += dot(rows, d[:, i * half : (i + 1) * half].reshape(SEQ * half, DPACK), 0, 0)
    send_ref[...] = (grad / TOTAL).astype(BF16)
    tail = jnp.sum(d[:, :, 2 * N :].astype(F32), axis=0)
    low = iota((8, LANES), 1)
    out = jnp.zeros((8, LANES), F32)
    for k in range(HEAD):
        at = H if k < 4 else H + 16
        rolled = pltpu.roll(tail[8 * (k % 4) : 8 * (k % 4) + 8], (HEADS * k - at) % LANES, 1)
        mine = jnp.logical_and(low >= HEADS * k, low < HEADS * (k + 1))
        out += jnp.where(mine, rolled, 0.0)
    par_ref[...] = ((out[0:3] + out[3:6]) / TOTAL)[:, :H]


def add_kernel(a_ref, b_ref, out_ref):
    out_ref[...] = (a_ref[...].astype(F32) + b_ref[...].astype(F32)).astype(BF16)


def spread_kernel(a_ref, b_ref, send_ref):
    total = (a_ref[...].astype(F32) + b_ref[...].astype(F32)).astype(BF16)
    for s in range(SEQ):
        send_ref[s] = total


def unpack_kernel(r_ref, bc_hbm, dt_hbm, bc_ref, dt_ref, sems):
    parts = SEQ // STAGES
    copies = []
    for i in range(STAGES):
        part = r_ref[i * parts : (i + 1) * parts]
        at = slice(i * parts * COLS, (i + 1) * parts * COLS)
        bc_ref[at] = part[:, :, : 2 * N].astype(F32).reshape(parts * COLS, 2 * N)
        copies.append(pltpu.make_async_copy(bc_ref.at[at], bc_hbm.at[at], sems.at[i, 0]))
        copies[-1].start()
        dt_ref[:, at] = part[:, :, 2 * N :].astype(F32).reshape(parts * COLS, LANES).T[:H]
        copies.append(pltpu.make_async_copy(dt_ref.at[:, at], dt_hbm.at[:, at], sems.at[i, 1]))
        copies[-1].start()
    for copy in copies:
        copy.wait()


def call(kernel, outs, *args, scratch=(), far=False, far_out=False, limit=LIMIT):
    return pl.pallas_call(
        kernel,
        out_shape=[jax.ShapeDtypeStruct(shape, kind) for shape, kind in outs],
        in_specs=[pl.BlockSpec(memory_space=pltpu.HBM if far else pltpu.VMEM)] * len(args),
        out_specs=[pl.BlockSpec(memory_space=pltpu.HBM if far_out else pltpu.VMEM)] * len(outs),
        scratch_shapes=list(scratch),
        compiler_params=pltpu.CompilerParams(vmem_limit_bytes=limit),
    )(*args)


def unpack(w_all):
    return pl.pallas_call(
        unpack_kernel,
        out_shape=[jax.ShapeDtypeStruct((D, 2 * N), F32), jax.ShapeDtypeStruct((H, D), F32)],
        in_specs=[pl.BlockSpec(memory_space=pltpu.VMEM)],
        out_specs=[pl.BlockSpec(memory_space=pltpu.HBM)] * 2,
        scratch_shapes=[
            pltpu.VMEM((D, 2 * N), F32),
            pltpu.VMEM((H, D), F32),
            pltpu.SemaphoreType.DMA((STAGES, 2)),
        ],
        compiler_params=pltpu.CompilerParams(vmem_limit_bytes=LIMIT),
    )(w_all)


def exchange(v, axis):
    return lax.all_to_all(v, axis, split_axis=0, concat_axis=0, tiled=True)


def per_device(hidden, x_input, grad_out, bc_weight, dt_weight, dt_bias, a_log, d_skip):
    prm = jnp.pad(jnp.stack([dt_bias, a_log, d_skip]), ((0, 5), (0, LANES - H)))
    [packed] = call(
        project_kernel,
        [((HEAD, TOKENS, PACK), BF16)],
        hidden, bc_weight, dt_weight.T, x_input, grad_out,
        scratch=[
            pltpu.VMEM((HEAD, TOKENS, PACK), BF16),
            pltpu.VMEM((TOKENS, H * WIDTH), BF16),
            pltpu.VMEM((TOKENS, H * WIDTH), BF16),
            pltpu.VMEM((TOKENS, D), BF16),
            pltpu.VMEM((D, 2 * N), BF16),
            pltpu.VMEM((H, D), BF16),
            pltpu.SemaphoreType.DMA((8,)),
        ],
        far=True,
        far_out=True,
        limit=FULL,
    )
    mine = exchange(packed, "head").reshape(SPAN, PACK)
    [hid_send] = call(slab_kernel, [((SEQ, TOKENS // 2, 3 * LANES), BF16)], hidden)
    [sent] = call(
        totals_kernel, [((SEQ, 2 * SLAB, CH + 3 * LANES), BF16)], mine, prm, hid_send
    )
    totals = exchange(sent, "seq")
    [inner] = call(
        inner_kernel,
        [((SPAN, PACK + LANES), F32)],
        mine, prm,
        scratch=[pltpu.VMEM((SPAN, SPAN), F32)],
    )
    totals, inner = lax.optimization_barrier((totals, inner))
    [states] = call(prefix_kernel, [((SEQ, 2 * SLAB, CH), BF16)], totals)
    states = exchange(states, "seq")
    d_part, both = call(
        carry_kernel,
        [((HEAD, TOKENS, DPACK), BF16), ((SPAN, 2 * CH), BF16)],
        mine, prm, states, inner,
    )
    d_part = exchange(d_part, "head")
    [d_send] = call(
        reduce_kernel,
        [((SEQ, TOKENS, DPACK), BF16)],
        d_part,
    )
    d_all = exchange(d_send, "seq")
    [grad_hidden] = call(
        hidden_kernel, [((TOKENS, D), BF16)], d_send, bc_weight, dt_weight.T
    )
    d_all, grad_hidden = lax.optimization_barrier((d_all, grad_hidden))
    w_part, param_grads = call(
        weight_kernel, [((COLS, DPACK), BF16), ((3, H), F32)], d_all, totals
    )
    for far in (1, 2):
        other = lax.ppermute(w_part, "head", [(i, i ^ far) for i in range(HEAD)])
        [w_part] = call(add_kernel, [((COLS, DPACK), BF16)], w_part, other)
    other = lax.ppermute(w_part, "head", [(i, i ^ 4) for i in range(HEAD)])
    [w_sum] = call(
        spread_kernel,
        [((SEQ, COLS, DPACK), BF16)],
        w_part, other,
        limit=NEAR,
    )
    w_sum, both = lax.optimization_barrier((w_sum, both))
    w_all = exchange(w_sum, "seq")
    blocks = list(call(rotate_kernel, [((TOKENS, 2 * CH), BF16)] * HEAD, both))
    for k in range(1, HEAD):
        ring = [(i, (i + k) % HEAD) for i in range(HEAD)]
        blocks[k] = lax.ppermute(blocks[k], "head", ring)
    mixer_out, grad_x = call(
        finish_kernel, [((TOKENS, H * WIDTH), BF16)] * 2, *blocks
    )
    grad_bc_weight, grad_dt_weight = unpack(w_all)
    return (mixer_out, grad_x, grad_hidden, grad_bc_weight, grad_dt_weight.T, param_grads)


def solution(mesh):
    rows = P(("dp", "seq", "head"), None)
    return jax.shard_map(
        per_device,
        mesh=mesh,
        in_specs=(rows, rows, rows, P(), P(), P(), P(), P()),
        out_specs=(rows, rows, rows, P("dp", None), P("dp", None), P("dp", None)),
        check_vma=False,
    )
```

```python
import functools

import jax
import jax.numpy as jnp
from jax import lax
from jax.experimental import pallas as pl
from jax.experimental.pallas import tpu as pltpu
from jax.sharding import PartitionSpec as P

F32 = jnp.float32
BF16 = jnp.bfloat16
LANES = 128
LIMIT = 24 * 2**20
NEAR = 52 * 2**20
FULL = 60 * 2**20

SEQ, HEAD = 16, 8
D, H, WIDTH, N = 2560, 80, 64, 128
TOKENS = 32
SPAN = TOKENS * HEAD
HEADS = H // HEAD
CH = HEADS * WIDTH
TOTAL = SPAN * SEQ
COLS = D // SEQ
PACK = 2 * CH + 2 * N + LANES
DPACK = 2 * N + LANES
STEPS = (0, 4, 3, 5, 2, 6, 1, 7)
STAGES = 4
SLAB = N // SEQ
STEP = 2 * CH + 2 * N


def dot(a, b, ca=1, cb=0):
    return lax.dot_general(a, b, (((ca,), (cb,)), ((), ())), preferred_element_type=F32)


def iota(shape, dim):
    return lax.broadcasted_iota(jnp.int32, shape, dim)


def split(v, parts):
    out = []
    for _ in range(parts):
        top = v.astype(BF16)
        out.append(top)
        v = v - top.astype(F32)
    return out


def one_hot(shift=0):
    return (iota((LANES, CH), 0) - shift == iota((LANES, CH), 1) // WIDTH).astype(F32).astype(BF16)


def spread(v, hot):
    hi, lo = split(v, 2)
    return dot(hi, hot) + dot(lo, hot)


def gather_heads(v, hot, parts=2):
    return sum(dot(part, hot, 1, 1) for part in split(v, parts))


def triangle(dim):
    return (iota((SPAN, SPAN), dim) >= iota((SPAN, SPAN), 1 - dim)).astype(F32).astype(BF16)


def running_sum(tri, v):
    return sum(dot(tri, part) for part in split(v, 3))


def head_params(prm_ref):
    prm = pltpu.roll(prm_ref[...], lax.rem(LANES - HEADS * lax.axis_index("head"), LANES), 1)
    return prm[0:1], -jnp.exp(prm[1:2]), prm[2:3]


def step_sizes(r_ref, prm_ref, cum=None):
    bias, rate, skip = head_params(prm_ref)
    pre = r_ref[:, STEP:].astype(F32) + bias
    step = jnp.maximum(pre, 0.0) + jnp.log1p(jnp.exp(-jnp.abs(pre)))
    if cum is None:
        cum = running_sum(triangle(0), step * rate)
    return pre, step, cum, rate, skip


def project_kernel(
    hid_hbm, wbc_hbm, wdt_hbm, x_hbm, g_hbm, send_hbm, pack_ref, x_ref, g_ref, hid_ref, wbc_ref, wdt_ref, sems
):
    half = D // 2
    halves = [slice(0, half), slice(half, D)]
    come = [
        pltpu.make_async_copy(far, near, sems.at[i])
        for i, (far, near) in enumerate(
            [(x_hbm, x_ref), (g_hbm, g_ref), (hid_hbm, hid_ref), (wdt_hbm, wdt_ref)]
            + [(wbc_hbm.at[at], wbc_ref.at[at]) for at in halves]
        )
    ]
    go = [
        pltpu.make_async_copy(pack_ref.at[:, :, at], send_hbm.at[:, :, at], sems.at[len(come) + i])
        for i, at in enumerate((slice(0, 2 * CH), slice(2 * CH, PACK)))
    ]
    for copy in come:
        copy.start()
    for i, ref in enumerate((x_ref, g_ref)):
        come[i].wait()
        for k in range(HEAD):
            pack_ref[k, :, i * CH : (i + 1) * CH] = ref[:, k * CH : (k + 1) * CH]
    go[0].start()
    come[2].wait()
    come[3].wait()
    raw = dot(hid_ref[...], wdt_ref[...], 1, 1).astype(BF16).astype(F32)
    raw = jnp.concatenate([raw, jnp.zeros((TOKENS, LANES - H), F32)], axis=1)
    lane = iota((TOKENS, LANES), 1)
    for k in range(HEAD):
        mine = pltpu.roll(raw, (LANES - HEADS * k) % LANES, 1)
        pack_ref[k, :, STEP:] = jnp.where(lane < HEADS, mine, 0.0).astype(BF16)
    bc = jnp.zeros((TOKENS, 2 * N), F32)
    for i, at in enumerate(halves):
        come[4 + i].wait()
        bc += dot(hid_ref[:, at], wbc_ref[at])
    for k in range(HEAD):
        pack_ref[k, :, 2 * CH : STEP] = bc.astype(BF16)
    go[1].start()
    for copy in go:
        copy.wait()


def slab_kernel(hid_ref, hs_ref):
    half = TOKENS // 2
    wide = hid_ref[...].astype(F32)
    pad = jnp.zeros((half, 3 * LANES - 2 * COLS), F32)
    for s in range(SEQ):
        part = wide[:, s * COLS : (s + 1) * COLS]
        hs_ref[s] = jnp.concatenate([part[:half], part[half:], pad], axis=1).astype(BF16)


def totals_kernel(r_ref, prm_ref, hs_ref, send_ref):
    pre, step, cum, rate, skip = step_sizes(r_ref, prm_ref)
    hot = one_hot()
    total = cum[SPAN - 1 :]
    to_end = spread(step * jnp.exp(total - cum), hot)
    from_start = spread(jnp.exp(cum), hot)
    x = r_ref[:, :CH].astype(F32)
    g = r_ref[:, CH : 2 * CH].astype(F32)
    b = r_ref[:, 2 * CH : 2 * CH + N]
    c = r_ref[:, 2 * CH + N : STEP]
    fresh = dot(b, (x * to_end).astype(BF16), 0, 0)
    back = dot(c, (g * from_start).astype(BF16), 0, 0)
    both = jnp.concatenate(
        [fresh.reshape(SEQ, SLAB, CH), back.reshape(SEQ, SLAB, CH)], axis=1
    )
    send_ref[:, :, :CH] = both.astype(BF16)
    hi, lo = split(jnp.exp(total), 2)
    row = iota((2 * SLAB, LANES), 0)
    lane = iota((2 * SLAB, LANES), 1)
    decay = jnp.where(row == 0, hi.astype(F32), jnp.where(row == 1, lo.astype(F32), 0.0))
    decay = pltpu.roll(jnp.where(lane < HEADS, decay, 0.0), WIDTH, 1)
    send_ref[:, :, CH : CH + 2 * LANES] = hs_ref[:, :, : 2 * LANES]
    tail = hs_ref[:, :, 2 * LANES :].astype(F32) + decay[None]
    send_ref[:, :, CH + 2 * LANES :] = tail.astype(BF16)


def prefix_kernel(r_ref, out_ref):
    hot = one_hot(WIDTH)
    tail = r_ref[:, :, CH + 2 * LANES :].astype(F32)
    decay = dot(tail[:, 0, :].astype(BF16), hot) + dot(tail[:, 1, :].astype(BF16), hot)
    ahead, behind = [], [None] * SEQ
    state = jnp.zeros((SLAB, CH), F32)
    for s in range(SEQ):
        ahead.append(state)
        state = decay[s : s + 1] * state + r_ref[s, :, :CH].astype(F32)[:SLAB]
    state = jnp.zeros((SLAB, CH), F32)
    for s in reversed(range(SEQ)):
        behind[s] = state
        state = decay[s : s + 1] * state + r_ref[s, :, :CH].astype(F32)[SLAB:]
    for s in range(SEQ):
        out_ref[s] = jnp.concatenate([ahead[s], behind[s]], axis=0).astype(BF16)


def inner_kernel(r_ref, prm_ref, out_ref, ds_ref):
    pre, step, cum, rate, skip = step_sizes(r_ref, prm_ref)
    hot = one_hot()
    cum_t = cum.T
    b = r_ref[:, 2 * CH : 2 * CH + N]
    c = r_ref[:, 2 * CH + N : STEP]
    scores = dot(c, b, 1, 1)
    causal = iota((SPAN, SPAN), 0) >= iota((SPAN, SPAN), 1)
    step_x = spread(step, hot)
    low = iota((SPAN, LANES), 1) < WIDTH
    zero = jnp.zeros((SPAN, LANES), BF16)
    products = []
    for j in range(HEADS // 2):
        at = slice(j * LANES, (j + 1) * LANES)
        g = r_ref[:, CH + j * LANES : CH + (j + 1) * LANES]
        u = (r_ref[:, at].astype(F32) * step_x[:, at]).astype(BF16)
        g_t = g.astype(F32).T.astype(BF16)
        y = jnp.zeros((SPAN, LANES), F32)
        du_t = []
        for i in range(2):
            h = 2 * j + i
            mine = low if i == 0 else jnp.logical_not(low)
            gap = jnp.where(causal, cum[:, h : h + 1] - cum_t[h : h + 1, :], -1e30)
            decay = jnp.exp(gap)
            mixer = (decay * scores).astype(BF16)
            y += dot(mixer, jnp.where(mine, u, zero))
            du_t.append(dot(g_t[i * WIDTH : (i + 1) * WIDTH], mixer))
            d_mixer = dot(jnp.where(mine, g, zero), u, 1, 1) * decay
            if h == 0:
                ds_ref[...] = d_mixer
            else:
                ds_ref[...] += d_mixer
        du = jnp.concatenate(du_t, axis=0).T
        out_ref[:, at] = y
        out_ref[:, CH + j * LANES : CH + (j + 1) * LANES] = du
        products.append(g.astype(F32) * y - u.astype(F32) * du)
    out_ref[:, PACK:] = cum
    out_ref[:, STEP:PACK] = gather_heads(jnp.concatenate(products, axis=1), hot, 3)
    ds = ds_ref[...]
    out_ref[:, 2 * CH : 2 * CH + N] = dot(ds.T.astype(BF16), c)
    out_ref[:, 2 * CH + N : STEP] = dot(ds.astype(BF16), b)


def carry_kernel(r_ref, prm_ref, st_ref, in_ref, send_ref, both_ref):
    pre, step, cum, rate, skip = step_sizes(r_ref, prm_ref, in_ref[:, PACK:])
    hot = one_hot()
    total = cum[SPAN - 1 :]
    step_x = spread(step, hot)
    to_end = spread(jnp.exp(total - cum), hot)
    from_start = spread(jnp.exp(cum), hot)
    skip_x = spread(jnp.broadcast_to(skip, (8, LANES)), hot)[:1]
    states = st_ref[...].astype(F32)
    state_in = states[:, :SLAB].reshape(N, CH)
    state_gr = states[:, SLAB:].reshape(N, CH)
    x = r_ref[:, :CH].astype(F32)
    g = r_ref[:, CH : 2 * CH].astype(F32)
    b = r_ref[:, 2 * CH : 2 * CH + N]
    c = r_ref[:, 2 * CH + N : STEP]
    s_b = state_in.astype(BF16)
    q_b = state_gr.astype(BF16)
    u = x * step_x
    carried = dot(c, s_b) * from_start
    late = dot(b, q_b) * to_end
    y = in_ref[:, :CH] + carried + skip_x * x
    du = in_ref[:, CH : 2 * CH] + late
    gx = step_x * du + skip_x * g
    d_c = in_ref[:, 2 * CH + N : STEP] + dot((g * from_start).astype(BF16), s_b, 1, 1)
    d_b = in_ref[:, 2 * CH : 2 * CH + N] + dot((u * to_end).astype(BF16), q_b, 1, 1)
    e = in_ref[:, STEP:PACK] + gather_heads(g * carried, hot)
    f = gather_heads(u * late, hot)
    xdu = gather_heads(x * du, hot)
    sums = jnp.concatenate(
        [
            jnp.sum(state_in * state_gr, axis=0, keepdims=True),
            jnp.sum(g * x, axis=0, keepdims=True),
            jnp.zeros((6, CH), F32),
        ],
        axis=0,
    )
    sums = gather_heads(sums, hot, 3)
    edge = jnp.exp(total) * sums[0:1]
    d_rate = running_sum(triangle(1), e) + running_sum(triangle(0), f) - f + edge
    d_raw = (rate * d_rate + xdu) / (1.0 + jnp.exp(-pre))
    d_bias = jnp.sum(d_raw, axis=0, keepdims=True)
    d_log = rate * jnp.sum(step * d_rate, axis=0, keepdims=True)
    hi, lo = split(jnp.concatenate([d_bias, d_log, sums[1:2]], axis=0), 2)
    row = jnp.concatenate(
        [hi.astype(F32), lo.astype(F32), jnp.zeros((TOKENS - 6, LANES), F32)], axis=0
    )
    lane = iota((TOKENS, LANES), 1)
    row = pltpu.roll(jnp.where(lane < HEADS, row, 0.0), 16, 1)
    both_ref[:, :CH] = y.astype(BF16)
    both_ref[:, CH:] = gx.astype(BF16)
    for k in range(HEAD):
        at = slice(k * TOKENS, (k + 1) * TOKENS)
        send_ref[k, :, :N] = d_b[at].astype(BF16)
        send_ref[k, :, N : 2 * N] = d_c[at].astype(BF16)
        send_ref[k, :, 2 * N :] = (jnp.where(lane < HEADS, d_raw[at], 0.0) + row).astype(BF16)


def rotate_kernel(both_ref, *blocks):
    for k, block in zip(STEPS, blocks):
        to = lax.rem(lax.axis_index("head") + k, HEAD)
        block[...] = both_ref[pl.ds(pl.multiple_of(to * TOKENS, TOKENS), TOKENS), :]


def reduce_kernel(r_ref, send_ref):
    d_bc = jnp.sum(r_ref[:, :, : 2 * N].astype(F32), axis=0).astype(BF16)
    lane = iota((TOKENS, LANES), 1)
    steps = jnp.zeros((TOKENS, LANES), F32)
    rows = [[], []]
    low = iota((8, LANES), 1)
    for k in range(HEAD):
        tile = r_ref[k, :, 2 * N :].astype(F32)
        steps += pltpu.roll(jnp.where(lane < HEADS, tile, 0.0), HEADS * k, 1)
        mine = jnp.where(jnp.logical_and(low >= 16, low < 16 + HEADS), tile[:8], 0.0)
        rows[k // 4].append(pltpu.roll(mine, H - 16 if k < 4 else H, 1))
    tail = steps + jnp.concatenate(rows[0], axis=0) + jnp.concatenate(rows[1], axis=0)
    tail = tail.astype(BF16)
    for s in range(SEQ):
        send_ref[s, :, : 2 * N] = d_bc
        send_ref[s, :, 2 * N :] = tail


def hidden_kernel(d_ref, wbc_ref, wdt_ref, gh_ref):
    d_bc = d_ref[0, :, : 2 * N]
    d_step = d_ref[0, :, 2 * N :][:, :H]
    gh = dot(d_bc, wbc_ref[...], 1, 1) + dot(d_step, wdt_ref[...])
    gh_ref[...] = gh.astype(BF16)


def finish_kernel(*refs):
    blocks, outs = refs[:HEAD], refs[HEAD:]
    for k, block in zip(STEPS, blocks):
        of = lax.rem(lax.axis_index("head") + HEAD - k, HEAD)
        cols = pl.ds(pl.multiple_of(of * CH, LANES), CH)
        for i, out_ref in enumerate(outs):
            out_ref[:, cols] = block[:, i * CH : (i + 1) * CH]


def weight_kernel(d_ref, h_ref, send_ref, par_ref):
    half = TOKENS // 2
    d = d_ref[...]
    h = h_ref[:, :, CH:].astype(F32)
    grad = jnp.zeros((COLS, DPACK), F32)
    for i in range(2):
        rows = h[:, :, i * COLS : (i + 1) * COLS].reshape(SEQ * half, COLS).astype(BF16)
        grad += dot(rows, d[:, i * half : (i + 1) * half].reshape(SEQ * half, DPACK), 0, 0)
    send_ref[...] = (grad / TOTAL).astype(BF16)
    tail = jnp.sum(d[:, :, 2 * N :].astype(F32), axis=0)
    low = iota((8, LANES), 1)
    out = jnp.zeros((8, LANES), F32)
    for k in range(HEAD):
        at = H if k < 4 else H + 16
        rolled = pltpu.roll(tail[8 * (k % 4) : 8 * (k % 4) + 8], (HEADS * k - at) % LANES, 1)
        mine = jnp.logical_and(low >= HEADS * k, low < HEADS * (k + 1))
        out += jnp.where(mine, rolled, 0.0)
    par_ref[...] = ((out[0:3] + out[3:6]) / TOTAL)[:, :H]


def add_kernel(a_ref, b_ref, out_ref):
    out_ref[...] = (a_ref[...].astype(F32) + b_ref[...].astype(F32)).astype(BF16)


def spread_kernel(a_ref, b_ref, send_ref):
    total = (a_ref[...].astype(F32) + b_ref[...].astype(F32)).astype(BF16)
    for s in range(SEQ):
        send_ref[s] = total


def unpack_kernel(r_ref, bc_hbm, dt_hbm, bc_ref, dt_ref, sems):
    parts = SEQ // STAGES
    copies = []
    for i in range(STAGES):
        part = r_ref[i * parts : (i + 1) * parts]
        at = slice(i * parts * COLS, (i + 1) * parts * COLS)
        bc_ref[at] = part[:, :, : 2 * N].astype(F32).reshape(parts * COLS, 2 * N)
        copies.append(pltpu.make_async_copy(bc_ref.at[at], bc_hbm.at[at], sems.at[i, 0]))
        copies[-1].start()
        dt_ref[:, at] = part[:, :, 2 * N :].astype(F32).reshape(parts * COLS, LANES).T[:H]
        copies.append(pltpu.make_async_copy(dt_ref.at[:, at], dt_hbm.at[:, at], sems.at[i, 1]))
        copies[-1].start()
    for copy in copies:
        copy.wait()


def call(kernel, outs, *args, scratch=(), far=False, far_out=False, limit=LIMIT):
    return pl.pallas_call(
        kernel,
        out_shape=[jax.ShapeDtypeStruct(shape, kind) for shape, kind in outs],
        in_specs=[pl.BlockSpec(memory_space=pltpu.HBM if far else pltpu.VMEM)] * len(args),
        out_specs=[pl.BlockSpec(memory_space=pltpu.HBM if far_out else pltpu.VMEM)] * len(outs),
        scratch_shapes=list(scratch),
        compiler_params=pltpu.CompilerParams(vmem_limit_bytes=limit),
    )(*args)


def unpack(w_all):
    return pl.pallas_call(
        unpack_kernel,
        out_shape=[jax.ShapeDtypeStruct((D, 2 * N), F32), jax.ShapeDtypeStruct((H, D), F32)],
        in_specs=[pl.BlockSpec(memory_space=pltpu.VMEM)],
        out_specs=[pl.BlockSpec(memory_space=pltpu.HBM)] * 2,
        scratch_shapes=[
            pltpu.VMEM((D, 2 * N), F32),
            pltpu.VMEM((H, D), F32),
            pltpu.SemaphoreType.DMA((STAGES, 2)),
        ],
        compiler_params=pltpu.CompilerParams(vmem_limit_bytes=LIMIT),
    )(w_all)


def exchange(v, axis):
    return lax.all_to_all(v, axis, split_axis=0, concat_axis=0, tiled=True)


def per_device(hidden, x_input, grad_out, bc_weight, dt_weight, dt_bias, a_log, d_skip):
    prm = jnp.pad(jnp.stack([dt_bias, a_log, d_skip]), ((0, 5), (0, LANES - H)))
    [packed] = call(
        project_kernel,
        [((HEAD, TOKENS, PACK), BF16)],
        hidden, bc_weight, dt_weight.T, x_input, grad_out,
        scratch=[
            pltpu.VMEM((HEAD, TOKENS, PACK), BF16),
            pltpu.VMEM((TOKENS, H * WIDTH), BF16),
            pltpu.VMEM((TOKENS, H * WIDTH), BF16),
            pltpu.VMEM((TOKENS, D), BF16),
            pltpu.VMEM((D, 2 * N), BF16),
            pltpu.VMEM((H, D), BF16),
            pltpu.SemaphoreType.DMA((8,)),
        ],
        far=True,
        far_out=True,
        limit=FULL,
    )
    mine = exchange(packed, "head").reshape(SPAN, PACK)
    [hid_send] = call(slab_kernel, [((SEQ, TOKENS // 2, 3 * LANES), BF16)], hidden)
    [sent] = call(
        totals_kernel, [((SEQ, 2 * SLAB, CH + 3 * LANES), BF16)], mine, prm, hid_send
    )
    totals = exchange(sent, "seq")
    [inner] = call(
        inner_kernel,
        [((SPAN, PACK + LANES), F32)],
        mine, prm,
        scratch=[pltpu.VMEM((SPAN, SPAN), F32)],
    )
    totals, inner = lax.optimization_barrier((totals, inner))
    [states] = call(prefix_kernel, [((SEQ, 2 * SLAB, CH), BF16)], totals)
    states = exchange(states, "seq")
    d_part, both = call(
        carry_kernel,
        [((HEAD, TOKENS, DPACK), BF16), ((SPAN, 2 * CH), BF16)],
        mine, prm, states, inner,
    )
    d_part = exchange(d_part, "head")
    [d_send] = call(
        reduce_kernel,
        [((SEQ, TOKENS, DPACK), BF16)],
        d_part,
    )
    d_all = exchange(d_send, "seq")
    [grad_hidden] = call(
        hidden_kernel, [((TOKENS, D), BF16)], d_send, bc_weight, dt_weight.T
    )
    d_all, grad_hidden = lax.optimization_barrier((d_all, grad_hidden))
    w_part, param_grads = call(
        weight_kernel, [((COLS, DPACK), BF16), ((3, H), F32)], d_all, totals
    )
    for far in (1, 2):
        other = lax.ppermute(w_part, "head", [(i, i ^ far) for i in range(HEAD)])
        [w_part] = call(add_kernel, [((COLS, DPACK), BF16)], w_part, other)
    other = lax.ppermute(w_part, "head", [(i, i ^ 7) for i in range(HEAD)])
    [w_sum] = call(
        spread_kernel,
        [((SEQ, COLS, DPACK), BF16)],
        w_part, other,
        limit=NEAR,
    )
    w_sum, both = lax.optimization_barrier((w_sum, both))
    w_all = exchange(w_sum, "seq")
    blocks = list(call(rotate_kernel, [((TOKENS, 2 * CH), BF16)] * HEAD, both))
    for j, k in enumerate(STEPS):
        if k > 0:
            ring = [(i, (i + k) % HEAD) for i in range(HEAD)]
            blocks[j] = lax.ppermute(blocks[j], "head", ring)
    mixer_out, grad_x = call(
        finish_kernel, [((TOKENS, H * WIDTH), BF16)] * 2, *blocks
    )
    grad_bc_weight, grad_dt_weight = unpack(w_all)
    return (mixer_out, grad_x, grad_hidden, grad_bc_weight, grad_dt_weight.T, param_grads)


def solution(mesh):
    rows = P(("dp", "seq", "head"), None)
    return jax.shard_map(
        per_device,
        mesh=mesh,
        in_specs=(rows, rows, rows, P(), P(), P(), P(), P()),
        out_specs=(rows, rows, rows, P("dp", None), P("dp", None), P("dp", None)),
        check_vma=False,
    )
```

```python
import functools

import jax
import jax.numpy as jnp
from jax import lax
from jax.experimental import pallas as pl
from jax.experimental.pallas import tpu as pltpu
from jax.sharding import PartitionSpec as P

F32 = jnp.float32
BF16 = jnp.bfloat16
LANES = 128
LIMIT = 24 * 2**20
NEAR = 52 * 2**20
FULL = 60 * 2**20

SEQ, HEAD = 16, 8
D, H, WIDTH, N = 2560, 80, 64, 128
TOKENS = 32
SPAN = TOKENS * HEAD
HEADS = H // HEAD
CH = HEADS * WIDTH
TOTAL = SPAN * SEQ
COLS = D // SEQ
PACK = 2 * CH + 2 * N + LANES
DPACK = 2 * N + LANES
FOLD = 24
ROWS = 2 * COLS + COLS // 2 + FOLD + 8
STEPS = (0, 4, 3, 5, 2, 6, 1, 7)
STAGES = 4
SLAB = N // SEQ
STEP = 2 * CH + 2 * N


def dot(a, b, ca=1, cb=0):
    return lax.dot_general(a, b, (((ca,), (cb,)), ((), ())), preferred_element_type=F32)


def iota(shape, dim):
    return lax.broadcasted_iota(jnp.int32, shape, dim)


def split(v, parts):
    out = []
    for _ in range(parts):
        top = v.astype(BF16)
        out.append(top)
        v = v - top.astype(F32)
    return out


def one_hot(shift=0):
    return (iota((LANES, CH), 0) - shift == iota((LANES, CH), 1) // WIDTH).astype(F32).astype(BF16)


def spread(v, hot):
    hi, lo = split(v, 2)
    return dot(hi, hot) + dot(lo, hot)


def gather_heads(v, hot, parts=2):
    return sum(dot(part, hot, 1, 1) for part in split(v, parts))


def triangle(dim):
    return (iota((SPAN, SPAN), dim) >= iota((SPAN, SPAN), 1 - dim)).astype(F32).astype(BF16)


def running_sum(tri, v):
    return sum(dot(tri, part) for part in split(v, 3))


def head_params(prm_ref):
    prm = pltpu.roll(prm_ref[...], lax.rem(LANES - HEADS * lax.axis_index("head"), LANES), 1)
    return prm[0:1], -jnp.exp(prm[1:2]), prm[2:3]


def step_sizes(r_ref, prm_ref, cum=None):
    bias, rate, skip = head_params(prm_ref)
    pre = r_ref[:, STEP:].astype(F32) + bias
    step = jnp.maximum(pre, 0.0) + jnp.log1p(jnp.exp(-jnp.abs(pre)))
    if cum is None:
        cum = running_sum(triangle(0), step * rate)
    return pre, step, cum, rate, skip


def project_kernel(
    hid_hbm, wbc_hbm, wdt_hbm, x_hbm, g_hbm, send_hbm, pack_ref, x_ref, g_ref, hid_ref, wbc_ref, wdt_ref, sems
):
    half = D // 2
    halves = [slice(0, half), slice(half, D)]
    come = [
        pltpu.make_async_copy(far, near, sems.at[i])
        for i, (far, near) in enumerate(
            [(x_hbm, x_ref), (g_hbm, g_ref), (hid_hbm, hid_ref), (wdt_hbm, wdt_ref)]
            + [(wbc_hbm.at[at], wbc_ref.at[at]) for at in halves]
        )
    ]
    go = [
        pltpu.make_async_copy(pack_ref.at[:, :, at], send_hbm.at[:, :, at], sems.at[len(come) + i])
        for i, at in enumerate((slice(0, 2 * CH), slice(2 * CH, PACK)))
    ]
    for copy in come:
        copy.start()
    for i, ref in enumerate((x_ref, g_ref)):
        come[i].wait()
        for k in range(HEAD):
            pack_ref[k, :, i * CH : (i + 1) * CH] = ref[:, k * CH : (k + 1) * CH]
    go[0].start()
    come[2].wait()
    come[3].wait()
    raw = dot(hid_ref[...], wdt_ref[...], 1, 1).astype(BF16).astype(F32)
    raw = jnp.concatenate([raw, jnp.zeros((TOKENS, LANES - H), F32)], axis=1)
    lane = iota((TOKENS, LANES), 1)
    for k in range(HEAD):
        mine = pltpu.roll(raw, (LANES - HEADS * k) % LANES, 1)
        pack_ref[k, :, STEP:] = jnp.where(lane < HEADS, mine, 0.0).astype(BF16)
    bc = jnp.zeros((TOKENS, 2 * N), F32)
    for i, at in enumerate(halves):
        come[4 + i].wait()
        bc += dot(hid_ref[:, at], wbc_ref[at])
    for k in range(HEAD):
        pack_ref[k, :, 2 * CH : STEP] = bc.astype(BF16)
    go[1].start()
    for copy in go:
        copy.wait()


def slab_kernel(hid_ref, hs_ref):
    half = TOKENS // 2
    wide = hid_ref[...].astype(F32)
    pad = jnp.zeros((half, 3 * LANES - 2 * COLS), F32)
    for s in range(SEQ):
        part = wide[:, s * COLS : (s + 1) * COLS]
        hs_ref[s] = jnp.concatenate([part[:half], part[half:], pad], axis=1).astype(BF16)


def totals_kernel(r_ref, prm_ref, hs_ref, send_ref):
    pre, step, cum, rate, skip = step_sizes(r_ref, prm_ref)
    hot = one_hot()
    total = cum[SPAN - 1 :]
    to_end = spread(step * jnp.exp(total - cum), hot)
    from_start = spread(jnp.exp(cum), hot)
    x = r_ref[:, :CH].astype(F32)
    g = r_ref[:, CH : 2 * CH].astype(F32)
    b = r_ref[:, 2 * CH : 2 * CH + N]
    c = r_ref[:, 2 * CH + N : STEP]
    fresh = dot(b, (x * to_end).astype(BF16), 0, 0)
    back = dot(c, (g * from_start).astype(BF16), 0, 0)
    both = jnp.concatenate(
        [fresh.reshape(SEQ, SLAB, CH), back.reshape(SEQ, SLAB, CH)], axis=1
    )
    send_ref[:, :, :CH] = both.astype(BF16)
    hi, lo = split(jnp.exp(total), 2)
    row = iota((2 * SLAB, LANES), 0)
    lane = iota((2 * SLAB, LANES), 1)
    decay = jnp.where(row == 0, hi.astype(F32), jnp.where(row == 1, lo.astype(F32), 0.0))
    decay = pltpu.roll(jnp.where(lane < HEADS, decay, 0.0), WIDTH, 1)
    send_ref[:, :, CH : CH + 2 * LANES] = hs_ref[:, :, : 2 * LANES]
    tail = hs_ref[:, :, 2 * LANES :].astype(F32) + decay[None]
    send_ref[:, :, CH + 2 * LANES :] = tail.astype(BF16)


def prefix_kernel(r_ref, out_ref):
    hot = one_hot(WIDTH)
    tail = r_ref[:, :, CH + 2 * LANES :].astype(F32)
    decay = dot(tail[:, 0, :].astype(BF16), hot) + dot(tail[:, 1, :].astype(BF16), hot)
    ahead, behind = [], [None] * SEQ
    state = jnp.zeros((SLAB, CH), F32)
    for s in range(SEQ):
        ahead.append(state)
        state = decay[s : s + 1] * state + r_ref[s, :, :CH].astype(F32)[:SLAB]
    state = jnp.zeros((SLAB, CH), F32)
    for s in reversed(range(SEQ)):
        behind[s] = state
        state = decay[s : s + 1] * state + r_ref[s, :, :CH].astype(F32)[SLAB:]
    for s in range(SEQ):
        out_ref[s] = jnp.concatenate([ahead[s], behind[s]], axis=0).astype(BF16)


def inner_kernel(r_ref, prm_ref, out_ref, ds_ref):
    pre, step, cum, rate, skip = step_sizes(r_ref, prm_ref)
    hot = one_hot()
    cum_t = cum.T
    b = r_ref[:, 2 * CH : 2 * CH + N]
    c = r_ref[:, 2 * CH + N : STEP]
    scores = dot(c, b, 1, 1)
    causal = iota((SPAN, SPAN), 0) >= iota((SPAN, SPAN), 1)
    step_x = spread(step, hot)
    low = iota((SPAN, LANES), 1) < WIDTH
    zero = jnp.zeros((SPAN, LANES), BF16)
    products = []
    for j in range(HEADS // 2):
        at = slice(j * LANES, (j + 1) * LANES)
        g = r_ref[:, CH + j * LANES : CH + (j + 1) * LANES]
        u = (r_ref[:, at].astype(F32) * step_x[:, at]).astype(BF16)
        g_t = g.astype(F32).T.astype(BF16)
        y = jnp.zeros((SPAN, LANES), F32)
        du_t = []
        for i in range(2):
            h = 2 * j + i
            mine = low if i == 0 else jnp.logical_not(low)
            gap = jnp.where(causal, cum[:, h : h + 1] - cum_t[h : h + 1, :], -1e30)
            decay = jnp.exp(gap)
            mixer = (decay * scores).astype(BF16)
            y += dot(mixer, jnp.where(mine, u, zero))
            du_t.append(dot(g_t[i * WIDTH : (i + 1) * WIDTH], mixer))
            d_mixer = dot(jnp.where(mine, g, zero), u, 1, 1) * decay
            if h == 0:
                ds_ref[...] = d_mixer
            else:
                ds_ref[...] += d_mixer
        du = jnp.concatenate(du_t, axis=0).T
        out_ref[:, at] = y
        out_ref[:, CH + j * LANES : CH + (j + 1) * LANES] = du
        products.append(g.astype(F32) * y - u.astype(F32) * du)
    out_ref[:, PACK:] = cum
    out_ref[:, STEP:PACK] = gather_heads(jnp.concatenate(products, axis=1), hot, 3)
    ds = ds_ref[...]
    out_ref[:, 2 * CH : 2 * CH + N] = dot(ds.T.astype(BF16), c)
    out_ref[:, 2 * CH + N : STEP] = dot(ds.astype(BF16), b)


def carry_kernel(r_ref, prm_ref, st_ref, in_ref, send_ref, both_ref):
    pre, step, cum, rate, skip = step_sizes(r_ref, prm_ref, in_ref[:, PACK:])
    hot = one_hot()
    total = cum[SPAN - 1 :]
    step_x = spread(step, hot)
    to_end = spread(jnp.exp(total - cum), hot)
    from_start = spread(jnp.exp(cum), hot)
    skip_x = spread(jnp.broadcast_to(skip, (8, LANES)), hot)[:1]
    states = st_ref[...].astype(F32)
    state_in = states[:, :SLAB].reshape(N, CH)
    state_gr = states[:, SLAB:].reshape(N, CH)
    x = r_ref[:, :CH].astype(F32)
    g = r_ref[:, CH : 2 * CH].astype(F32)
    b = r_ref[:, 2 * CH : 2 * CH + N]
    c = r_ref[:, 2 * CH + N : STEP]
    s_b = state_in.astype(BF16)
    q_b = state_gr.astype(BF16)
    u = x * step_x
    carried = dot(c, s_b) * from_start
    late = dot(b, q_b) * to_end
    y = in_ref[:, :CH] + carried + skip_x * x
    du = in_ref[:, CH : 2 * CH] + late
    gx = step_x * du + skip_x * g
    d_c = in_ref[:, 2 * CH + N : STEP] + dot((g * from_start).astype(BF16), s_b, 1, 1)
    d_b = in_ref[:, 2 * CH : 2 * CH + N] + dot((u * to_end).astype(BF16), q_b, 1, 1)
    e = in_ref[:, STEP:PACK] + gather_heads(g * carried, hot)
    f = gather_heads(u * late, hot)
    xdu = gather_heads(x * du, hot)
    sums = jnp.concatenate(
        [
            jnp.sum(state_in * state_gr, axis=0, keepdims=True),
            jnp.sum(g * x, axis=0, keepdims=True),
            jnp.zeros((6, CH), F32),
        ],
        axis=0,
    )
    sums = gather_heads(sums, hot, 3)
    edge = jnp.exp(total) * sums[0:1]
    d_rate = running_sum(triangle(1), e) + running_sum(triangle(0), f) - f + edge
    d_raw = (rate * d_rate + xdu) / (1.0 + jnp.exp(-pre))
    d_bias = jnp.sum(d_raw, axis=0, keepdims=True)
    d_log = rate * jnp.sum(step * d_rate, axis=0, keepdims=True)
    hi, lo = split(jnp.concatenate([d_bias, d_log, sums[1:2]], axis=0), 2)
    row = jnp.concatenate(
        [hi.astype(F32), lo.astype(F32), jnp.zeros((TOKENS - 6, LANES), F32)], axis=0
    )
    lane = iota((TOKENS, LANES), 1)
    row = pltpu.roll(jnp.where(lane < HEADS, row, 0.0), 16, 1)
    both_ref[:, :CH] = y.astype(BF16)
    both_ref[:, CH:] = gx.astype(BF16)
    for k in range(HEAD):
        at = slice(k * TOKENS, (k + 1) * TOKENS)
        send_ref[k, :, :N] = d_b[at].astype(BF16)
        send_ref[k, :, N : 2 * N] = d_c[at].astype(BF16)
        send_ref[k, :, 2 * N :] = (jnp.where(lane < HEADS, d_raw[at], 0.0) + row).astype(BF16)


def rotate_kernel(both_ref, *blocks):
    for k, block in zip(STEPS, blocks):
        to = lax.rem(lax.axis_index("head") + k, HEAD)
        block[...] = both_ref[pl.ds(pl.multiple_of(to * TOKENS, TOKENS), TOKENS), :]


def reduce_kernel(r_ref, send_ref):
    d_bc = jnp.sum(r_ref[:, :, : 2 * N].astype(F32), axis=0).astype(BF16)
    lane = iota((TOKENS, LANES), 1)
    steps = jnp.zeros((TOKENS, LANES), F32)
    rows = [[], []]
    low = iota((8, LANES), 1)
    for k in range(HEAD):
        tile = r_ref[k, :, 2 * N :].astype(F32)
        steps += pltpu.roll(jnp.where(lane < HEADS, tile, 0.0), HEADS * k, 1)
        mine = jnp.where(jnp.logical_and(low >= 16, low < 16 + HEADS), tile[:8], 0.0)
        rows[k // 4].append(pltpu.roll(mine, H - 16 if k < 4 else H, 1))
    tail = steps + jnp.concatenate(rows[0], axis=0) + jnp.concatenate(rows[1], axis=0)
    tail = tail.astype(BF16)
    for s in range(SEQ):
        send_ref[s, :, : 2 * N] = d_bc
        send_ref[s, :, 2 * N :] = tail


def hidden_kernel(d_ref, wbc_ref, wdt_ref, gh_ref):
    d_bc = d_ref[0, :, : 2 * N]
    d_step = d_ref[0, :, 2 * N :][:, :H]
    gh = dot(d_bc, wbc_ref[...], 1, 1) + dot(d_step, wdt_ref[...])
    gh_ref[...] = gh.astype(BF16)


def finish_kernel(*refs):
    blocks, outs = refs[:HEAD], refs[HEAD:]
    for k, block in zip(STEPS, blocks):
        of = lax.rem(lax.axis_index("head") + HEAD - k, HEAD)
        cols = pl.ds(pl.multiple_of(of * CH, LANES), CH)
        for i, out_ref in enumerate(outs):
            out_ref[:, cols] = block[:, i * CH : (i + 1) * CH]


def fold(grad):
    half, cut = COLS // 2, LANES // 2
    steps = grad[:, 2 * N :]
    lane = iota((half, LANES), 1)
    wide = jnp.where(lane < cut, steps[:half], pltpu.roll(steps[half:], cut, 1))
    padded = jnp.concatenate([steps, jnp.zeros((-COLS % FOLD, LANES), F32)], axis=0)
    rest = jnp.zeros((FOLD, LANES), F32)
    lane = iota((FOLD, LANES), 1)
    for j in range(padded.shape[0] // FOLD):
        piece = padded[j * FOLD : (j + 1) * FOLD]
        piece = jnp.where(jnp.logical_and(lane >= cut, lane < H), piece, 0.0)
        rest += pltpu.roll(piece, (cut + (H - cut) * j) % LANES, 1)
    return jnp.concatenate(
        [grad[:, :N], grad[:, N : 2 * N], wide, rest, jnp.zeros((8, LANES), F32)], axis=0
    )


def unfold_steps(packed):
    half, cut = COLS // 2, LANES // 2
    tail = packed[2 * COLS :].astype(F32)
    wide, rest = tail[:half], tail[half : half + FOLD]
    low = jnp.concatenate([wide, pltpu.roll(wide, cut, 1)], axis=0)
    high = [
        pltpu.roll(rest, (2 * LANES - cut - (H - cut) * j) % LANES, 1)
        for j in range(-(-COLS // FOLD))
    ]
    high = jnp.concatenate(high, axis=0)[:COLS]
    return jnp.where(iota((COLS, LANES), 1) < cut, low, high)


def weight_kernel(d_ref, h_ref, send_ref, par_ref):
    half = TOKENS // 2
    d = d_ref[...]
    h = h_ref[:, :, CH:].astype(F32)
    grad = jnp.zeros((COLS, DPACK), F32)
    for i in range(2):
        rows = h[:, :, i * COLS : (i + 1) * COLS].reshape(SEQ * half, COLS).astype(BF16)
        grad += dot(rows, d[:, i * half : (i + 1) * half].reshape(SEQ * half, DPACK), 0, 0)
    send_ref[...] = fold(grad / TOTAL).astype(BF16)
    tail = jnp.sum(d[:, :, 2 * N :].astype(F32), axis=0)
    low = iota((8, LANES), 1)
    out = jnp.zeros((8, LANES), F32)
    for k in range(HEAD):
        at = H if k < 4 else H + 16
        rolled = pltpu.roll(tail[8 * (k % 4) : 8 * (k % 4) + 8], (HEADS * k - at) % LANES, 1)
        mine = jnp.logical_and(low >= HEADS * k, low < HEADS * (k + 1))
        out += jnp.where(mine, rolled, 0.0)
    par_ref[...] = ((out[0:3] + out[3:6]) / TOTAL)[:, :H]


def add_kernel(a_ref, b_ref, out_ref):
    out_ref[...] = (a_ref[...].astype(F32) + b_ref[...].astype(F32)).astype(BF16)


def spread_kernel(a_ref, b_ref, send_ref):
    total = (a_ref[...].astype(F32) + b_ref[...].astype(F32)).astype(BF16)
    for s in range(SEQ):
        send_ref[s] = total


def unpack_kernel(r_ref, bc_hbm, dt_hbm, bc_ref, dt_ref, sems):
    parts = SEQ // STAGES
    copies = []
    for i in range(STAGES):
        part = range(i * parts, (i + 1) * parts)
        at = slice(i * parts * COLS, (i + 1) * parts * COLS)
        for s in part:
            rows = slice(s * COLS, (s + 1) * COLS)
            bc_ref[rows, :N] = r_ref[s, :COLS].astype(F32)
            bc_ref[rows, N:] = r_ref[s, COLS : 2 * COLS].astype(F32)
        copies.append(pltpu.make_async_copy(bc_ref.at[at], bc_hbm.at[at], sems.at[i, 0]))
        copies[-1].start()
        steps = jnp.concatenate([unfold_steps(r_ref[s]) for s in part], axis=0)
        dt_ref[:, at] = steps.T[:H]
        copies.append(pltpu.make_async_copy(dt_ref.at[:, at], dt_hbm.at[:, at], sems.at[i, 1]))
        copies[-1].start()
    for copy in copies:
        copy.wait()


def call(kernel, outs, *args, scratch=(), far=False, far_out=False, limit=LIMIT):
    return pl.pallas_call(
        kernel,
        out_shape=[jax.ShapeDtypeStruct(shape, kind) for shape, kind in outs],
        in_specs=[pl.BlockSpec(memory_space=pltpu.HBM if far else pltpu.VMEM)] * len(args),
        out_specs=[pl.BlockSpec(memory_space=pltpu.HBM if far_out else pltpu.VMEM)] * len(outs),
        scratch_shapes=list(scratch),
        compiler_params=pltpu.CompilerParams(vmem_limit_bytes=limit),
    )(*args)


def unpack(w_all):
    return pl.pallas_call(
        unpack_kernel,
        out_shape=[jax.ShapeDtypeStruct((D, 2 * N), F32), jax.ShapeDtypeStruct((H, D), F32)],
        in_specs=[pl.BlockSpec(memory_space=pltpu.VMEM)],
        out_specs=[pl.BlockSpec(memory_space=pltpu.HBM)] * 2,
        scratch_shapes=[
            pltpu.VMEM((D, 2 * N), F32),
            pltpu.VMEM((H, D), F32),
            pltpu.SemaphoreType.DMA((STAGES, 2)),
        ],
        compiler_params=pltpu.CompilerParams(vmem_limit_bytes=LIMIT),
    )(w_all)


def exchange(v, axis):
    return lax.all_to_all(v, axis, split_axis=0, concat_axis=0, tiled=True)


def per_device(hidden, x_input, grad_out, bc_weight, dt_weight, dt_bias, a_log, d_skip):
    prm = jnp.pad(jnp.stack([dt_bias, a_log, d_skip]), ((0, 5), (0, LANES - H)))
    [packed] = call(
        project_kernel,
        [((HEAD, TOKENS, PACK), BF16)],
        hidden, bc_weight, dt_weight.T, x_input, grad_out,
        scratch=[
            pltpu.VMEM((HEAD, TOKENS, PACK), BF16),
            pltpu.VMEM((TOKENS, H * WIDTH), BF16),
            pltpu.VMEM((TOKENS, H * WIDTH), BF16),
            pltpu.VMEM((TOKENS, D), BF16),
            pltpu.VMEM((D, 2 * N), BF16),
            pltpu.VMEM((H, D), BF16),
            pltpu.SemaphoreType.DMA((8,)),
        ],
        far=True,
        far_out=True,
        limit=FULL,
    )
    mine = exchange(packed, "head").reshape(SPAN, PACK)
    [hid_send] = call(slab_kernel, [((SEQ, TOKENS // 2, 3 * LANES), BF16)], hidden)
    [sent] = call(
        totals_kernel, [((SEQ, 2 * SLAB, CH + 3 * LANES), BF16)], mine, prm, hid_send
    )
    totals = exchange(sent, "seq")
    [inner] = call(
        inner_kernel,
        [((SPAN, PACK + LANES), F32)],
        mine, prm,
        scratch=[pltpu.VMEM((SPAN, SPAN), F32)],
    )
    totals, inner = lax.optimization_barrier((totals, inner))
    [states] = call(prefix_kernel, [((SEQ, 2 * SLAB, CH), BF16)], totals)
    states = exchange(states, "seq")
    d_part, both = call(
        carry_kernel,
        [((HEAD, TOKENS, DPACK), BF16), ((SPAN, 2 * CH), BF16)],
        mine, prm, states, inner,
    )
    d_part = exchange(d_part, "head")
    [d_send] = call(
        reduce_kernel,
        [((SEQ, TOKENS, DPACK), BF16)],
        d_part,
    )
    d_all = exchange(d_send, "seq")
    [grad_hidden] = call(
        hidden_kernel, [((TOKENS, D), BF16)], d_send, bc_weight, dt_weight.T
    )
    d_all, grad_hidden = lax.optimization_barrier((d_all, grad_hidden))
    w_part, param_grads = call(
        weight_kernel, [((ROWS, LANES), BF16), ((3, H), F32)], d_all, totals
    )
    for far in (1, 2):
        other = lax.ppermute(w_part, "head", [(i, i ^ far) for i in range(HEAD)])
        [w_part] = call(add_kernel, [((ROWS, LANES), BF16)], w_part, other)
    other = lax.ppermute(w_part, "head", [(i, i ^ 7) for i in range(HEAD)])
    [w_sum] = call(
        spread_kernel,
        [((SEQ, ROWS, LANES), BF16)],
        w_part, other,
        limit=NEAR,
    )
    w_sum, both = lax.optimization_barrier((w_sum, both))
    w_all = exchange(w_sum, "seq")
    blocks = list(call(rotate_kernel, [((TOKENS, 2 * CH), BF16)] * HEAD, both))
    for j, k in enumerate(STEPS):
        if k > 0:
            ring = [(i, (i + k) % HEAD) for i in range(HEAD)]
            blocks[j] = lax.ppermute(blocks[j], "head", ring)
    mixer_out, grad_x = call(
        finish_kernel, [((TOKENS, H * WIDTH), BF16)] * 2, *blocks
    )
    grad_bc_weight, grad_dt_weight = unpack(w_all)
    return (mixer_out, grad_x, grad_hidden, grad_bc_weight, grad_dt_weight.T, param_grads)


def solution(mesh):
    rows = P(("dp", "seq", "head"), None)
    return jax.shard_map(
        per_device,
        mesh=mesh,
        in_specs=(rows, rows, rows, P(), P(), P(), P(), P()),
        out_specs=(rows, rows, rows, P("dp", None), P("dp", None), P("dp", None)),
        check_vma=False,
    )
```

```python
import functools

import jax
import jax.numpy as jnp
from jax import lax
from jax.experimental import pallas as pl
from jax.experimental.pallas import tpu as pltpu
from jax.sharding import PartitionSpec as P

F32 = jnp.float32
BF16 = jnp.bfloat16
LANES = 128
LIMIT = 24 * 2**20
NEAR = 52 * 2**20
FULL = 60 * 2**20

SEQ, HEAD = 16, 8
D, H, WIDTH, N = 2560, 80, 64, 128
TOKENS = 32
SPAN = TOKENS * HEAD
HEADS = H // HEAD
CH = HEADS * WIDTH
TOTAL = SPAN * SEQ
COLS = D // SEQ
PACK = 2 * CH + 2 * N + LANES
DPACK = 2 * N + LANES
FOLD = 24
ROWS = 2 * COLS + COLS // 2 + FOLD + 8
STEPS = (0, 4, 3, 5, 2, 6, 1, 7)
STAGES = 4
SLAB = N // SEQ
STEP = 2 * CH + 2 * N


def dot(a, b, ca=1, cb=0):
    return lax.dot_general(a, b, (((ca,), (cb,)), ((), ())), preferred_element_type=F32)


def iota(shape, dim):
    return lax.broadcasted_iota(jnp.int32, shape, dim)


def split(v, parts):
    out = []
    for _ in range(parts):
        top = v.astype(BF16)
        out.append(top)
        v = v - top.astype(F32)
    return out


def one_hot(shift=0):
    return (iota((LANES, CH), 0) - shift == iota((LANES, CH), 1) // WIDTH).astype(F32).astype(BF16)


def spread(v, hot):
    hi, lo = split(v, 2)
    return dot(hi, hot) + dot(lo, hot)


def gather_heads(v, hot, parts=2):
    return sum(dot(part, hot, 1, 1) for part in split(v, parts))


def triangle(dim):
    return (iota((SPAN, SPAN), dim) >= iota((SPAN, SPAN), 1 - dim)).astype(F32).astype(BF16)


def running_sum(tri, v):
    return sum(dot(tri, part) for part in split(v, 3))


def head_params(prm_ref):
    prm = pltpu.roll(prm_ref[...], lax.rem(LANES - HEADS * lax.axis_index("head"), LANES), 1)
    return prm[0:1], -jnp.exp(prm[1:2]), prm[2:3]


def step_sizes(r_ref, prm_ref, cum=None):
    bias, rate, skip = head_params(prm_ref)
    pre = r_ref[:, STEP:].astype(F32) + bias
    step = jnp.maximum(pre, 0.0) + jnp.log1p(jnp.exp(-jnp.abs(pre)))
    if cum is None:
        cum = running_sum(triangle(0), step * rate)
    return pre, step, cum, rate, skip


def project_kernel(
    hid_hbm, wbc_hbm, wdt_hbm, x_hbm, g_hbm, send_hbm, pack_ref, x_ref, g_ref, hid_ref, wbc_ref, wdt_ref, sems
):
    half = D // 2
    halves = [slice(0, half), slice(half, D)]
    come = [
        pltpu.make_async_copy(far, near, sems.at[i])
        for i, (far, near) in enumerate(
            [(x_hbm, x_ref), (g_hbm, g_ref), (hid_hbm, hid_ref), (wdt_hbm, wdt_ref)]
            + [(wbc_hbm.at[at], wbc_ref.at[at]) for at in halves]
        )
    ]
    go = [
        pltpu.make_async_copy(pack_ref.at[:, :, at], send_hbm.at[:, :, at], sems.at[len(come) + i])
        for i, at in enumerate((slice(0, 2 * CH), slice(2 * CH, PACK)))
    ]
    for copy in come:
        copy.start()
    for i, ref in enumerate((x_ref, g_ref)):
        come[i].wait()
        for k in range(HEAD):
            pack_ref[k, :, i * CH : (i + 1) * CH] = ref[:, k * CH : (k + 1) * CH]
    go[0].start()
    come[2].wait()
    come[3].wait()
    raw = dot(hid_ref[...], wdt_ref[...], 1, 1).astype(BF16).astype(F32)
    raw = jnp.concatenate([raw, jnp.zeros((TOKENS, LANES - H), F32)], axis=1)
    lane = iota((TOKENS, LANES), 1)
    for k in range(HEAD):
        mine = pltpu.roll(raw, (LANES - HEADS * k) % LANES, 1)
        pack_ref[k, :, STEP:] = jnp.where(lane < HEADS, mine, 0.0).astype(BF16)
    bc = jnp.zeros((TOKENS, 2 * N), F32)
    for i, at in enumerate(halves):
        come[4 + i].wait()
        bc += dot(hid_ref[:, at], wbc_ref[at])
    for k in range(HEAD):
        pack_ref[k, :, 2 * CH : STEP] = bc.astype(BF16)
    go[1].start()
    for copy in go:
        copy.wait()


def slab_kernel(hid_ref, hs_ref):
    half = TOKENS // 2
    wide = hid_ref[...].astype(F32)
    pad = jnp.zeros((half, 3 * LANES - 2 * COLS), F32)
    for s in range(SEQ):
        part = wide[:, s * COLS : (s + 1) * COLS]
        hs_ref[s] = jnp.concatenate([part[:half], part[half:], pad], axis=1).astype(BF16)


def totals_kernel(r_ref, prm_ref, hs_ref, send_ref):
    pre, step, cum, rate, skip = step_sizes(r_ref, prm_ref)
    hot = one_hot()
    total = cum[SPAN - 1 :]
    to_end = spread(step * jnp.exp(total - cum), hot)
    from_start = spread(jnp.exp(cum), hot)
    x = r_ref[:, :CH].astype(F32)
    g = r_ref[:, CH : 2 * CH].astype(F32)
    b = r_ref[:, 2 * CH : 2 * CH + N]
    c = r_ref[:, 2 * CH + N : STEP]
    fresh = dot(b, (x * to_end).astype(BF16), 0, 0)
    back = dot(c, (g * from_start).astype(BF16), 0, 0)
    both = jnp.concatenate(
        [fresh.reshape(SEQ, SLAB, CH), back.reshape(SEQ, SLAB, CH)], axis=1
    )
    send_ref[:, :, :CH] = both.astype(BF16)
    hi, lo = split(jnp.exp(total), 2)
    row = iota((2 * SLAB, LANES), 0)
    lane = iota((2 * SLAB, LANES), 1)
    decay = jnp.where(row == 0, hi.astype(F32), jnp.where(row == 1, lo.astype(F32), 0.0))
    decay = pltpu.roll(jnp.where(lane < HEADS, decay, 0.0), WIDTH, 1)
    send_ref[:, :, CH : CH + 2 * LANES] = hs_ref[:, :, : 2 * LANES]
    tail = hs_ref[:, :, 2 * LANES :].astype(F32) + decay[None]
    send_ref[:, :, CH + 2 * LANES :] = tail.astype(BF16)


def prefix_kernel(r_ref, out_ref):
    hot = one_hot(WIDTH)
    tail = r_ref[:, :, CH + 2 * LANES :].astype(F32)
    decay = dot(tail[:, 0, :].astype(BF16), hot) + dot(tail[:, 1, :].astype(BF16), hot)
    ahead, behind = [], [None] * SEQ
    state = jnp.zeros((SLAB, CH), F32)
    for s in range(SEQ):
        ahead.append(state)
        state = decay[s : s + 1] * state + r_ref[s, :, :CH].astype(F32)[:SLAB]
    state = jnp.zeros((SLAB, CH), F32)
    for s in reversed(range(SEQ)):
        behind[s] = state
        state = decay[s : s + 1] * state + r_ref[s, :, :CH].astype(F32)[SLAB:]
    for s in range(SEQ):
        out_ref[s] = jnp.concatenate([ahead[s], behind[s]], axis=0).astype(BF16)


def inner_kernel(r_ref, prm_ref, out_ref, ds_ref):
    pre, step, cum, rate, skip = step_sizes(r_ref, prm_ref)
    hot = one_hot()
    cum_t = cum.T
    b = r_ref[:, 2 * CH : 2 * CH + N]
    c = r_ref[:, 2 * CH + N : STEP]
    scores = dot(c, b, 1, 1)
    causal = iota((SPAN, SPAN), 0) >= iota((SPAN, SPAN), 1)
    step_x = spread(step, hot)
    low = iota((SPAN, LANES), 1) < WIDTH
    zero = jnp.zeros((SPAN, LANES), BF16)
    products = []
    for j in range(HEADS // 2):
        at = slice(j * LANES, (j + 1) * LANES)
        g = r_ref[:, CH + j * LANES : CH + (j + 1) * LANES]
        u = (r_ref[:, at].astype(F32) * step_x[:, at]).astype(BF16)
        g_t = g.astype(F32).T.astype(BF16)
        y = jnp.zeros((SPAN, LANES), F32)
        du_t = []
        for i in range(2):
            h = 2 * j + i
            mine = low if i == 0 else jnp.logical_not(low)
            gap = jnp.where(causal, cum[:, h : h + 1] - cum_t[h : h + 1, :], -1e30)
            decay = jnp.exp(gap)
            mixer = (decay * scores).astype(BF16)
            y += dot(mixer, jnp.where(mine, u, zero))
            du_t.append(dot(g_t[i * WIDTH : (i + 1) * WIDTH], mixer))
            d_mixer = dot(jnp.where(mine, g, zero), u, 1, 1) * decay
            if h == 0:
                ds_ref[...] = d_mixer
            else:
                ds_ref[...] += d_mixer
        du = jnp.concatenate(du_t, axis=0).T
        out_ref[:, at] = y
        out_ref[:, CH + j * LANES : CH + (j + 1) * LANES] = du
        products.append(g.astype(F32) * y - u.astype(F32) * du)
    out_ref[:, PACK:] = cum
    out_ref[:, STEP:PACK] = gather_heads(jnp.concatenate(products, axis=1), hot, 3)
    ds = ds_ref[...]
    out_ref[:, 2 * CH : 2 * CH + N] = dot(ds.T.astype(BF16), c)
    out_ref[:, 2 * CH + N : STEP] = dot(ds.astype(BF16), b)


def carry_kernel(r_ref, prm_ref, st_ref, in_ref, send_ref, both_ref):
    pre, step, cum, rate, skip = step_sizes(r_ref, prm_ref, in_ref[:, PACK:])
    hot = one_hot()
    total = cum[SPAN - 1 :]
    step_x = spread(step, hot)
    to_end = spread(jnp.exp(total - cum), hot)
    from_start = spread(jnp.exp(cum), hot)
    skip_x = spread(jnp.broadcast_to(skip, (8, LANES)), hot)[:1]
    states = st_ref[...].astype(F32)
    state_in = states[:, :SLAB].reshape(N, CH)
    state_gr = states[:, SLAB:].reshape(N, CH)
    x = r_ref[:, :CH].astype(F32)
    g = r_ref[:, CH : 2 * CH].astype(F32)
    b = r_ref[:, 2 * CH : 2 * CH + N]
    c = r_ref[:, 2 * CH + N : STEP]
    s_b = state_in.astype(BF16)
    q_b = state_gr.astype(BF16)
    u = x * step_x
    carried = dot(c, s_b) * from_start
    late = dot(b, q_b) * to_end
    y = in_ref[:, :CH] + carried + skip_x * x
    du = in_ref[:, CH : 2 * CH] + late
    gx = step_x * du + skip_x * g
    d_c = in_ref[:, 2 * CH + N : STEP] + dot((g * from_start).astype(BF16), s_b, 1, 1)
    d_b = in_ref[:, 2 * CH : 2 * CH + N] + dot((u * to_end).astype(BF16), q_b, 1, 1)
    e = in_ref[:, STEP:PACK] + gather_heads(g * carried, hot)
    f = gather_heads(u * late, hot)
    xdu = gather_heads(x * du, hot)
    sums = jnp.concatenate(
        [
            jnp.sum(state_in * state_gr, axis=0, keepdims=True),
            jnp.sum(g * x, axis=0, keepdims=True),
            jnp.zeros((6, CH), F32),
        ],
        axis=0,
    )
    sums = gather_heads(sums, hot, 3)
    edge = jnp.exp(total) * sums[0:1]
    d_rate = running_sum(triangle(1), e) + running_sum(triangle(0), f) - f + edge
    d_raw = (rate * d_rate + xdu) / (1.0 + jnp.exp(-pre))
    d_bias = jnp.sum(d_raw, axis=0, keepdims=True)
    d_log = rate * jnp.sum(step * d_rate, axis=0, keepdims=True)
    hi, lo = split(jnp.concatenate([d_bias, d_log, sums[1:2]], axis=0), 2)
    row = jnp.concatenate(
        [hi.astype(F32), lo.astype(F32), jnp.zeros((TOKENS - 6, LANES), F32)], axis=0
    )
    lane = iota((TOKENS, LANES), 1)
    row = pltpu.roll(jnp.where(lane < HEADS, row, 0.0), 16, 1)
    both_ref[:, :CH] = y.astype(BF16)
    both_ref[:, CH:] = gx.astype(BF16)
    for k in range(HEAD):
        at = slice(k * TOKENS, (k + 1) * TOKENS)
        send_ref[k, :, :N] = d_b[at].astype(BF16)
        send_ref[k, :, N : 2 * N] = d_c[at].astype(BF16)
        send_ref[k, :, 2 * N :] = (jnp.where(lane < HEADS, d_raw[at], 0.0) + row).astype(BF16)


def rotate_kernel(both_ref, *blocks):
    for k, block in zip(STEPS, blocks):
        to = lax.rem(lax.axis_index("head") + k, HEAD)
        block[...] = both_ref[pl.ds(pl.multiple_of(to * TOKENS, TOKENS), TOKENS), :]


def reduce_kernel(r_ref, send_ref):
    d_bc = jnp.sum(r_ref[:, :, : 2 * N].astype(F32), axis=0).astype(BF16)
    lane = iota((TOKENS, LANES), 1)
    steps = jnp.zeros((TOKENS, LANES), F32)
    rows = [[], []]
    low = iota((8, LANES), 1)
    for k in range(HEAD):
        tile = r_ref[k, :, 2 * N :].astype(F32)
        steps += pltpu.roll(jnp.where(lane < HEADS, tile, 0.0), HEADS * k, 1)
        mine = jnp.where(jnp.logical_and(low >= 16, low < 16 + HEADS), tile[:8], 0.0)
        rows[k // 4].append(pltpu.roll(mine, H - 16 if k < 4 else H, 1))
    tail = steps + jnp.concatenate(rows[0], axis=0) + jnp.concatenate(rows[1], axis=0)
    tail = tail.astype(BF16)
    for s in range(SEQ):
        send_ref[s, :, : 2 * N] = d_bc
        send_ref[s, :, 2 * N :] = tail


def hidden_kernel(d_ref, wbc_ref, wdt_ref, gh_ref):
    d_bc = d_ref[0, :, : 2 * N]
    d_step = d_ref[0, :, 2 * N :][:, :H]
    gh = dot(d_bc, wbc_ref[...], 1, 1) + dot(d_step, wdt_ref[...])
    gh_ref[...] = gh.astype(BF16)


def finish_kernel(*refs):
    blocks, outs = refs[:HEAD], refs[HEAD:]
    for k, block in zip(STEPS, blocks):
        of = lax.rem(lax.axis_index("head") + HEAD - k, HEAD)
        cols = pl.ds(pl.multiple_of(of * CH, LANES), CH)
        for i, out_ref in enumerate(outs):
            out_ref[:, cols] = block[:, i * CH : (i + 1) * CH]


def fold(grad):
    half, cut = COLS // 2, LANES // 2
    steps = grad[:, 2 * N :]
    lane = iota((half, LANES), 1)
    wide = jnp.where(lane < cut, steps[:half], pltpu.roll(steps[half:], cut, 1))
    padded = jnp.concatenate([steps, jnp.zeros((-COLS % FOLD, LANES), F32)], axis=0)
    rest = jnp.zeros((FOLD, LANES), F32)
    lane = iota((FOLD, LANES), 1)
    for j in range(padded.shape[0] // FOLD):
        piece = padded[j * FOLD : (j + 1) * FOLD]
        piece = jnp.where(jnp.logical_and(lane >= cut, lane < H), piece, 0.0)
        rest += pltpu.roll(piece, (cut + (H - cut) * j) % LANES, 1)
    return jnp.concatenate(
        [grad[:, :N], grad[:, N : 2 * N], wide, rest, jnp.zeros((8, LANES), F32)], axis=0
    )


def unfold_steps(packed):
    half, cut = COLS // 2, LANES // 2
    tail = packed[2 * COLS :].astype(F32)
    wide, rest = tail[:half], tail[half : half + FOLD]
    low = jnp.concatenate([wide, pltpu.roll(wide, cut, 1)], axis=0)
    high = [
        pltpu.roll(rest, (2 * LANES - cut - (H - cut) * j) % LANES, 1)
        for j in range(-(-COLS // FOLD))
    ]
    high = jnp.concatenate(high, axis=0)[:COLS]
    return jnp.where(iota((COLS, LANES), 1) < cut, low, high)


def weight_kernel(d_ref, h_ref, send_ref, par_ref):
    half = TOKENS // 2
    d = d_ref[...]
    h = h_ref[:, :, CH:].astype(F32)
    grad = jnp.zeros((COLS, DPACK), F32)
    for i in range(2):
        rows = h[:, :, i * COLS : (i + 1) * COLS].reshape(SEQ * half, COLS).astype(BF16)
        grad += dot(rows, d[:, i * half : (i + 1) * half].reshape(SEQ * half, DPACK), 0, 0)
    send_ref[...] = fold(grad / TOTAL).astype(BF16)
    tail = jnp.sum(d[:, :, 2 * N :].astype(F32), axis=0)
    low = iota((8, LANES), 1)
    out = jnp.zeros((8, LANES), F32)
    for k in range(HEAD):
        at = H if k < 4 else H + 16
        rolled = pltpu.roll(tail[8 * (k % 4) : 8 * (k % 4) + 8], (HEADS * k - at) % LANES, 1)
        mine = jnp.logical_and(low >= HEADS * k, low < HEADS * (k + 1))
        out += jnp.where(mine, rolled, 0.0)
    par_ref[...] = ((out[0:3] + out[3:6]) / TOTAL)[:, :H]


def add_kernel(a_ref, b_ref, out_ref):
    out_ref[...] = (a_ref[...].astype(F32) + b_ref[...].astype(F32)).astype(BF16)


def spread_kernel(a_ref, b_ref, send_ref):
    total = (a_ref[...].astype(F32) + b_ref[...].astype(F32)).astype(BF16)
    for s in range(SEQ):
        send_ref[s] = total


def unpack_kernel(r_ref, bc_hbm, dt_hbm, bc_ref, dt_ref, sems):
    parts = SEQ // STAGES
    copies = []
    spans = [slice(i * parts * COLS, (i + 1) * parts * COLS) for i in range(STAGES)]
    for i, at in enumerate(spans):
        for s in range(i * parts, (i + 1) * parts):
            rows = slice(s * COLS, (s + 1) * COLS)
            bc_ref[rows, :N] = r_ref[s, :COLS].astype(F32)
            bc_ref[rows, N:] = r_ref[s, COLS : 2 * COLS].astype(F32)
        copies.append(pltpu.make_async_copy(bc_ref.at[at], bc_hbm.at[at], sems.at[i, 0]))
        copies[-1].start()
    for i, at in enumerate(spans):
        part = range(i * parts, (i + 1) * parts)
        steps = jnp.concatenate([unfold_steps(r_ref[s]) for s in part], axis=0)
        dt_ref[:, at] = steps.T[:H]
        copies.append(pltpu.make_async_copy(dt_ref.at[:, at], dt_hbm.at[:, at], sems.at[i, 1]))
        copies[-1].start()
    for copy in copies:
        copy.wait()


def call(kernel, outs, *args, scratch=(), far=False, far_out=False, limit=LIMIT):
    return pl.pallas_call(
        kernel,
        out_shape=[jax.ShapeDtypeStruct(shape, kind) for shape, kind in outs],
        in_specs=[pl.BlockSpec(memory_space=pltpu.HBM if far else pltpu.VMEM)] * len(args),
        out_specs=[pl.BlockSpec(memory_space=pltpu.HBM if far_out else pltpu.VMEM)] * len(outs),
        scratch_shapes=list(scratch),
        compiler_params=pltpu.CompilerParams(vmem_limit_bytes=limit),
    )(*args)


def unpack(w_all):
    return pl.pallas_call(
        unpack_kernel,
        out_shape=[jax.ShapeDtypeStruct((D, 2 * N), F32), jax.ShapeDtypeStruct((H, D), F32)],
        in_specs=[pl.BlockSpec(memory_space=pltpu.VMEM)],
        out_specs=[pl.BlockSpec(memory_space=pltpu.HBM)] * 2,
        scratch_shapes=[
            pltpu.VMEM((D, 2 * N), F32),
            pltpu.VMEM((H, D), F32),
            pltpu.SemaphoreType.DMA((STAGES, 2)),
        ],
        compiler_params=pltpu.CompilerParams(vmem_limit_bytes=LIMIT),
    )(w_all)


def exchange(v, axis):
    return lax.all_to_all(v, axis, split_axis=0, concat_axis=0, tiled=True)


def per_device(hidden, x_input, grad_out, bc_weight, dt_weight, dt_bias, a_log, d_skip):
    prm = jnp.pad(jnp.stack([dt_bias, a_log, d_skip]), ((0, 5), (0, LANES - H)))
    [packed] = call(
        project_kernel,
        [((HEAD, TOKENS, PACK), BF16)],
        hidden, bc_weight, dt_weight.T, x_input, grad_out,
        scratch=[
            pltpu.VMEM((HEAD, TOKENS, PACK), BF16),
            pltpu.VMEM((TOKENS, H * WIDTH), BF16),
            pltpu.VMEM((TOKENS, H * WIDTH), BF16),
            pltpu.VMEM((TOKENS, D), BF16),
            pltpu.VMEM((D, 2 * N), BF16),
            pltpu.VMEM((H, D), BF16),
            pltpu.SemaphoreType.DMA((8,)),
        ],
        far=True,
        far_out=True,
        limit=FULL,
    )
    mine = exchange(packed, "head").reshape(SPAN, PACK)
    [hid_send] = call(slab_kernel, [((SEQ, TOKENS // 2, 3 * LANES), BF16)], hidden)
    [sent] = call(
        totals_kernel, [((SEQ, 2 * SLAB, CH + 3 * LANES), BF16)], mine, prm, hid_send
    )
    totals = exchange(sent, "seq")
    [inner] = call(
        inner_kernel,
        [((SPAN, PACK + LANES), F32)],
        mine, prm,
        scratch=[pltpu.VMEM((SPAN, SPAN), F32)],
    )
    totals, inner = lax.optimization_barrier((totals, inner))
    [states] = call(prefix_kernel, [((SEQ, 2 * SLAB, CH), BF16)], totals)
    states = exchange(states, "seq")
    d_part, both = call(
        carry_kernel,
        [((HEAD, TOKENS, DPACK), BF16), ((SPAN, 2 * CH), BF16)],
        mine, prm, states, inner,
    )
    d_part = exchange(d_part, "head")
    [d_send] = call(
        reduce_kernel,
        [((SEQ, TOKENS, DPACK), BF16)],
        d_part,
    )
    d_all = exchange(d_send, "seq")
    [grad_hidden] = call(
        hidden_kernel, [((TOKENS, D), BF16)], d_send, bc_weight, dt_weight.T
    )
    d_all, grad_hidden = lax.optimization_barrier((d_all, grad_hidden))
    w_part, param_grads = call(
        weight_kernel, [((ROWS, LANES), BF16), ((3, H), F32)], d_all, totals
    )
    for far in (1, 2):
        other = lax.ppermute(w_part, "head", [(i, i ^ far) for i in range(HEAD)])
        [w_part] = call(add_kernel, [((ROWS, LANES), BF16)], w_part, other)
    other = lax.ppermute(w_part, "head", [(i, i ^ 7) for i in range(HEAD)])
    [w_sum] = call(
        spread_kernel,
        [((SEQ, ROWS, LANES), BF16)],
        w_part, other,
        limit=NEAR,
    )
    w_sum, both = lax.optimization_barrier((w_sum, both))
    w_all = exchange(w_sum, "seq")
    blocks = list(call(rotate_kernel, [((TOKENS, 2 * CH), BF16)] * HEAD, both))
    for j, k in enumerate(STEPS):
        if k > 0:
            ring = [(i, (i + k) % HEAD) for i in range(HEAD)]
            blocks[j] = lax.ppermute(blocks[j], "head", ring)
    mixer_out, grad_x = call(
        finish_kernel, [((TOKENS, H * WIDTH), BF16)] * 2, *blocks
    )
    grad_bc_weight, grad_dt_weight = unpack(w_all)
    return (mixer_out, grad_x, grad_hidden, grad_bc_weight, grad_dt_weight.T, param_grads)


def solution(mesh):
    rows = P(("dp", "seq", "head"), None)
    return jax.shard_map(
        per_device,
        mesh=mesh,
        in_specs=(rows, rows, rows, P(), P(), P(), P(), P()),
        out_specs=(rows, rows, rows, P("dp", None), P("dp", None), P("dp", None)),
        check_vma=False,
    )
```

```python
import functools

import jax
import jax.numpy as jnp
from jax import lax
from jax.experimental import pallas as pl
from jax.experimental.pallas import tpu as pltpu
from jax.sharding import PartitionSpec as P

F32 = jnp.float32
BF16 = jnp.bfloat16
LANES = 128
LIMIT = 24 * 2**20
NEAR = 52 * 2**20
FULL = 60 * 2**20

SEQ, HEAD = 16, 8
D, H, WIDTH, N = 2560, 80, 64, 128
TOKENS = 32
SPAN = TOKENS * HEAD
HEADS = H // HEAD
CH = HEADS * WIDTH
TOTAL = SPAN * SEQ
COLS = D // SEQ
PACK = 2 * CH + 2 * N + LANES
DPACK = 2 * N + LANES
FOLD = 24
ROWS = 2 * COLS + COLS // 2 + FOLD + 8
STEPS = (0, 4, 3, 5, 2, 6, 1, 7)
STAGES = 4
SLAB = N // SEQ
STEP = 2 * CH + 2 * N


def dot(a, b, ca=1, cb=0):
    return lax.dot_general(a, b, (((ca,), (cb,)), ((), ())), preferred_element_type=F32)


def iota(shape, dim):
    return lax.broadcasted_iota(jnp.int32, shape, dim)


def split(v, parts):
    out = []
    for _ in range(parts):
        top = v.astype(BF16)
        out.append(top)
        v = v - top.astype(F32)
    return out


def one_hot(shift=0):
    return (iota((LANES, CH), 0) - shift == iota((LANES, CH), 1) // WIDTH).astype(F32).astype(BF16)


def spread(v, hot):
    hi, lo = split(v, 2)
    return dot(hi, hot) + dot(lo, hot)


def gather_heads(v, hot, parts=2):
    return sum(dot(part, hot, 1, 1) for part in split(v, parts))


def triangle(dim):
    return (iota((SPAN, SPAN), dim) >= iota((SPAN, SPAN), 1 - dim)).astype(F32).astype(BF16)


def running_sum(tri, v):
    return sum(dot(tri, part) for part in split(v, 3))


def head_params(prm_ref):
    prm = pltpu.roll(prm_ref[...], lax.rem(LANES - HEADS * lax.axis_index("head"), LANES), 1)
    return prm[0:1], -jnp.exp(prm[1:2]), prm[2:3]


def step_sizes(r_ref, prm_ref, cum=None):
    bias, rate, skip = head_params(prm_ref)
    pre = r_ref[:, STEP:].astype(F32) + bias
    step = jnp.maximum(pre, 0.0) + jnp.log1p(jnp.exp(-jnp.abs(pre)))
    if cum is None:
        cum = running_sum(triangle(0), step * rate)
    return pre, step, cum, rate, skip


def project_kernel(
    hid_hbm, wbc_hbm, wdt_hbm, x_hbm, g_hbm, send_hbm, pack_ref, x_ref, g_ref, hid_ref, wbc_ref, wdt_ref, sems
):
    half = D // 2
    halves = [slice(0, half), slice(half, D)]
    come = [
        pltpu.make_async_copy(far, near, sems.at[i])
        for i, (far, near) in enumerate(
            [(x_hbm, x_ref), (g_hbm, g_ref), (hid_hbm, hid_ref), (wdt_hbm, wdt_ref)]
            + [(wbc_hbm.at[at], wbc_ref.at[at]) for at in halves]
        )
    ]
    go = [
        pltpu.make_async_copy(pack_ref.at[:, :, at], send_hbm.at[:, :, at], sems.at[len(come) + i])
        for i, at in enumerate((slice(0, 2 * CH), slice(2 * CH, PACK)))
    ]
    for copy in come:
        copy.start()
    for i, ref in enumerate((x_ref, g_ref)):
        come[i].wait()
        for k in range(HEAD):
            pack_ref[k, :, i * CH : (i + 1) * CH] = ref[:, k * CH : (k + 1) * CH]
    go[0].start()
    come[2].wait()
    come[3].wait()
    raw = dot(hid_ref[...], wdt_ref[...], 1, 1).astype(BF16).astype(F32)
    raw = jnp.concatenate([raw, jnp.zeros((TOKENS, LANES - H), F32)], axis=1)
    lane = iota((TOKENS, LANES), 1)
    for k in range(HEAD):
        mine = pltpu.roll(raw, (LANES - HEADS * k) % LANES, 1)
        pack_ref[k, :, STEP:] = jnp.where(lane < HEADS, mine, 0.0).astype(BF16)
    bc = jnp.zeros((TOKENS, 2 * N), F32)
    for i, at in enumerate(halves):
        come[4 + i].wait()
        bc += dot(hid_ref[:, at], wbc_ref[at])
    for k in range(HEAD):
        pack_ref[k, :, 2 * CH : STEP] = bc.astype(BF16)
    go[1].start()
    for copy in go:
        copy.wait()


def slab_kernel(hid_ref, hs_ref):
    half = TOKENS // 2
    wide = hid_ref[...].astype(F32)
    pad = jnp.zeros((half, 3 * LANES - 2 * COLS), F32)
    for s in range(SEQ):
        part = wide[:, s * COLS : (s + 1) * COLS]
        hs_ref[s] = jnp.concatenate([part[:half], part[half:], pad], axis=1).astype(BF16)


def totals_kernel(r_ref, prm_ref, hs_ref, send_ref):
    pre, step, cum, rate, skip = step_sizes(r_ref, prm_ref)
    hot = one_hot()
    total = cum[SPAN - 1 :]
    to_end = spread(step * jnp.exp(total - cum), hot)
    from_start = spread(jnp.exp(cum), hot)
    x = r_ref[:, :CH].astype(F32)
    g = r_ref[:, CH : 2 * CH].astype(F32)
    b = r_ref[:, 2 * CH : 2 * CH + N]
    c = r_ref[:, 2 * CH + N : STEP]
    fresh = dot(b, (x * to_end).astype(BF16), 0, 0)
    back = dot(c, (g * from_start).astype(BF16), 0, 0)
    both = jnp.concatenate(
        [fresh.reshape(SEQ, SLAB, CH), back.reshape(SEQ, SLAB, CH)], axis=1
    )
    send_ref[:, :, :CH] = both.astype(BF16)
    hi, lo = split(jnp.exp(total), 2)
    row = iota((2 * SLAB, LANES), 0)
    lane = iota((2 * SLAB, LANES), 1)
    decay = jnp.where(row == 0, hi.astype(F32), jnp.where(row == 1, lo.astype(F32), 0.0))
    decay = pltpu.roll(jnp.where(lane < HEADS, decay, 0.0), WIDTH, 1)
    send_ref[:, :, CH : CH + 2 * LANES] = hs_ref[:, :, : 2 * LANES]
    tail = hs_ref[:, :, 2 * LANES :].astype(F32) + decay[None]
    send_ref[:, :, CH + 2 * LANES :] = tail.astype(BF16)


def prefix_kernel(r_ref, out_ref):
    hot = one_hot(WIDTH)
    tail = r_ref[:, :, CH + 2 * LANES :].astype(F32)
    decay = dot(tail[:, 0, :].astype(BF16), hot) + dot(tail[:, 1, :].astype(BF16), hot)
    ahead, behind = [], [None] * SEQ
    state = jnp.zeros((SLAB, CH), F32)
    for s in range(SEQ):
        ahead.append(state)
        state = decay[s : s + 1] * state + r_ref[s, :, :CH].astype(F32)[:SLAB]
    state = jnp.zeros((SLAB, CH), F32)
    for s in reversed(range(SEQ)):
        behind[s] = state
        state = decay[s : s + 1] * state + r_ref[s, :, :CH].astype(F32)[SLAB:]
    for s in range(SEQ):
        out_ref[s] = jnp.concatenate([ahead[s], behind[s]], axis=0).astype(BF16)


def inner_kernel(r_ref, prm_ref, out_ref, ds_ref):
    pre, step, cum, rate, skip = step_sizes(r_ref, prm_ref)
    hot = one_hot()
    cum_t = cum.T
    b = r_ref[:, 2 * CH : 2 * CH + N]
    c = r_ref[:, 2 * CH + N : STEP]
    scores = dot(c, b, 1, 1)
    causal = iota((SPAN, SPAN), 0) >= iota((SPAN, SPAN), 1)
    step_x = spread(step, hot)
    low = iota((SPAN, LANES), 1) < WIDTH
    zero = jnp.zeros((SPAN, LANES), BF16)
    products = []
    for j in range(HEADS // 2):
        at = slice(j * LANES, (j + 1) * LANES)
        g = r_ref[:, CH + j * LANES : CH + (j + 1) * LANES]
        u = (r_ref[:, at].astype(F32) * step_x[:, at]).astype(BF16)
        g_t = g.astype(F32).T.astype(BF16)
        y = jnp.zeros((SPAN, LANES), F32)
        du_t = []
        for i in range(2):
            h = 2 * j + i
            mine = low if i == 0 else jnp.logical_not(low)
            gap = jnp.where(causal, cum[:, h : h + 1] - cum_t[h : h + 1, :], -1e30)
            decay = jnp.exp(gap)
            mixer = (decay * scores).astype(BF16)
            y += dot(mixer, jnp.where(mine, u, zero))
            du_t.append(dot(g_t[i * WIDTH : (i + 1) * WIDTH], mixer))
            d_mixer = dot(jnp.where(mine, g, zero), u, 1, 1) * decay
            if h == 0:
                ds_ref[...] = d_mixer
            else:
                ds_ref[...] += d_mixer
        du = jnp.concatenate(du_t, axis=0).T
        out_ref[:, at] = y
        out_ref[:, CH + j * LANES : CH + (j + 1) * LANES] = du
        products.append(g.astype(F32) * y - u.astype(F32) * du)
    out_ref[:, PACK:] = cum
    out_ref[:, STEP:PACK] = gather_heads(jnp.concatenate(products, axis=1), hot, 3)
    ds = ds_ref[...]
    out_ref[:, 2 * CH : 2 * CH + N] = dot(ds.T.astype(BF16), c)
    out_ref[:, 2 * CH + N : STEP] = dot(ds.astype(BF16), b)


def carry_kernel(r_ref, prm_ref, st_ref, in_ref, send_ref, both_ref):
    pre, step, cum, rate, skip = step_sizes(r_ref, prm_ref, in_ref[:, PACK:])
    hot = one_hot()
    total = cum[SPAN - 1 :]
    wide = spread(jnp.concatenate([step, jnp.exp(total - cum), jnp.exp(cum)], axis=0), hot)
    step_x, to_end, from_start = (wide[i * SPAN : (i + 1) * SPAN] for i in range(3))
    skip_x = spread(jnp.broadcast_to(skip, (8, LANES)), hot)[:1]
    states = st_ref[...].astype(F32)
    state_in = states[:, :SLAB].reshape(N, CH)
    state_gr = states[:, SLAB:].reshape(N, CH)
    x = r_ref[:, :CH].astype(F32)
    g = r_ref[:, CH : 2 * CH].astype(F32)
    b = r_ref[:, 2 * CH : 2 * CH + N]
    c = r_ref[:, 2 * CH + N : STEP]
    s_b = state_in.astype(BF16)
    q_b = state_gr.astype(BF16)
    u = x * step_x
    carried = dot(c, s_b) * from_start
    late = dot(b, q_b) * to_end
    y = in_ref[:, :CH] + carried + skip_x * x
    du = in_ref[:, CH : 2 * CH] + late
    gx = step_x * du + skip_x * g
    d_c = in_ref[:, 2 * CH + N : STEP] + dot((g * from_start).astype(BF16), s_b, 1, 1)
    d_b = in_ref[:, 2 * CH : 2 * CH + N] + dot((u * to_end).astype(BF16), q_b, 1, 1)
    narrow = gather_heads(jnp.concatenate([g * carried, u * late, x * du], axis=0), hot)
    e, f, xdu = (narrow[i * SPAN : (i + 1) * SPAN] for i in range(3))
    e += in_ref[:, STEP:PACK]
    sums = jnp.concatenate(
        [
            jnp.sum(state_in * state_gr, axis=0, keepdims=True),
            jnp.sum(g * x, axis=0, keepdims=True),
            jnp.zeros((6, CH), F32),
        ],
        axis=0,
    )
    sums = gather_heads(sums, hot, 3)
    edge = jnp.exp(total) * sums[0:1]
    d_rate = running_sum(triangle(1), e) + running_sum(triangle(0), f) - f + edge
    d_raw = (rate * d_rate + xdu) / (1.0 + jnp.exp(-pre))
    d_bias = jnp.sum(d_raw, axis=0, keepdims=True)
    d_log = rate * jnp.sum(step * d_rate, axis=0, keepdims=True)
    hi, lo = split(jnp.concatenate([d_bias, d_log, sums[1:2]], axis=0), 2)
    row = jnp.concatenate(
        [hi.astype(F32), lo.astype(F32), jnp.zeros((TOKENS - 6, LANES), F32)], axis=0
    )
    lane = iota((TOKENS, LANES), 1)
    row = pltpu.roll(jnp.where(lane < HEADS, row, 0.0), 16, 1)
    both_ref[:, :CH] = y.astype(BF16)
    both_ref[:, CH:] = gx.astype(BF16)
    for k in range(HEAD):
        at = slice(k * TOKENS, (k + 1) * TOKENS)
        send_ref[k, :, :N] = d_b[at].astype(BF16)
        send_ref[k, :, N : 2 * N] = d_c[at].astype(BF16)
        send_ref[k, :, 2 * N :] = (jnp.where(lane < HEADS, d_raw[at], 0.0) + row).astype(BF16)


def rotate_kernel(both_ref, *blocks):
    for k, block in zip(STEPS, blocks):
        to = lax.rem(lax.axis_index("head") + k, HEAD)
        block[...] = both_ref[pl.ds(pl.multiple_of(to * TOKENS, TOKENS), TOKENS), :]


def reduce_kernel(r_ref, send_ref):
    d_bc = jnp.sum(r_ref[:, :, : 2 * N].astype(F32), axis=0).astype(BF16)
    lane = iota((TOKENS, LANES), 1)
    steps = jnp.zeros((TOKENS, LANES), F32)
    rows = [[], []]
    low = iota((8, LANES), 1)
    for k in range(HEAD):
        tile = r_ref[k, :, 2 * N :].astype(F32)
        steps += pltpu.roll(jnp.where(lane < HEADS, tile, 0.0), HEADS * k, 1)
        mine = jnp.where(jnp.logical_and(low >= 16, low < 16 + HEADS), tile[:8], 0.0)
        rows[k // 4].append(pltpu.roll(mine, H - 16 if k < 4 else H, 1))
    tail = steps + jnp.concatenate(rows[0], axis=0) + jnp.concatenate(rows[1], axis=0)
    tail = tail.astype(BF16)
    for s in range(SEQ):
        send_ref[s, :, : 2 * N] = d_bc
        send_ref[s, :, 2 * N :] = tail


def hidden_kernel(d_ref, wbc_ref, wdt_ref, gh_ref):
    d_bc = d_ref[0, :, : 2 * N]
    d_step = d_ref[0, :, 2 * N :][:, :H]
    gh = dot(d_bc, wbc_ref[...], 1, 1) + dot(d_step, wdt_ref[...])
    gh_ref[...] = gh.astype(BF16)


def finish_kernel(*refs):
    blocks, outs = refs[:HEAD], refs[HEAD:]
    for k, block in zip(STEPS, blocks):
        of = lax.rem(lax.axis_index("head") + HEAD - k, HEAD)
        cols = pl.ds(pl.multiple_of(of * CH, LANES), CH)
        for i, out_ref in enumerate(outs):
            out_ref[:, cols] = block[:, i * CH : (i + 1) * CH]


def fold(grad):
    half, cut = COLS // 2, LANES // 2
    steps = grad[:, 2 * N :]
    lane = iota((half, LANES), 1)
    wide = jnp.where(lane < cut, steps[:half], pltpu.roll(steps[half:], cut, 1))
    padded = jnp.concatenate([steps, jnp.zeros((-COLS % FOLD, LANES), F32)], axis=0)
    rest = jnp.zeros((FOLD, LANES), F32)
    lane = iota((FOLD, LANES), 1)
    for j in range(padded.shape[0] // FOLD):
        piece = padded[j * FOLD : (j + 1) * FOLD]
        piece = jnp.where(jnp.logical_and(lane >= cut, lane < H), piece, 0.0)
        rest += pltpu.roll(piece, (cut + (H - cut) * j) % LANES, 1)
    return jnp.concatenate(
        [grad[:, :N], grad[:, N : 2 * N], wide, rest, jnp.zeros((8, LANES), F32)], axis=0
    )


def unfold_steps(packed):
    half, cut = COLS // 2, LANES // 2
    tail = packed[2 * COLS :].astype(F32)
    wide, rest = tail[:half], tail[half : half + FOLD]
    low = jnp.concatenate([wide, pltpu.roll(wide, cut, 1)], axis=0)
    high = [
        pltpu.roll(rest, (2 * LANES - cut - (H - cut) * j) % LANES, 1)
        for j in range(-(-COLS // FOLD))
    ]
    high = jnp.concatenate(high, axis=0)[:COLS]
    return jnp.where(iota((COLS, LANES), 1) < cut, low, high)


def weight_kernel(d_ref, h_ref, send_ref, par_ref):
    half = TOKENS // 2
    d = d_ref[...]
    h = h_ref[:, :, CH:].astype(F32)
    grad = jnp.zeros((COLS, DPACK), F32)
    for i in range(2):
        rows = h[:, :, i * COLS : (i + 1) * COLS].reshape(SEQ * half, COLS).astype(BF16)
        grad += dot(rows, d[:, i * half : (i + 1) * half].reshape(SEQ * half, DPACK), 0, 0)
    send_ref[...] = fold(grad / TOTAL).astype(BF16)
    tail = jnp.sum(d[:, :, 2 * N :].astype(F32), axis=0)
    low = iota((8, LANES), 1)
    out = jnp.zeros((8, LANES), F32)
    for k in range(HEAD):
        at = H if k < 4 else H + 16
        rolled = pltpu.roll(tail[8 * (k % 4) : 8 * (k % 4) + 8], (HEADS * k - at) % LANES, 1)
        mine = jnp.logical_and(low >= HEADS * k, low < HEADS * (k + 1))
        out += jnp.where(mine, rolled, 0.0)
    par_ref[...] = ((out[0:3] + out[3:6]) / TOTAL)[:, :H]


def add_kernel(a_ref, b_ref, out_ref):
    out_ref[...] = (a_ref[...].astype(F32) + b_ref[...].astype(F32)).astype(BF16)


def spread_kernel(a_ref, b_ref, send_ref):
    total = (a_ref[...].astype(F32) + b_ref[...].astype(F32)).astype(BF16)
    for s in range(SEQ):
        send_ref[s] = total


def unpack_kernel(r_ref, bc_hbm, dt_hbm, bc_ref, dt_ref, sems):
    parts = SEQ // STAGES
    copies = []
    for i in range(STAGES):
        part = range(i * parts, (i + 1) * parts)
        at = slice(i * parts * COLS, (i + 1) * parts * COLS)
        for s in part:
            rows = slice(s * COLS, (s + 1) * COLS)
            bc_ref[rows, :N] = r_ref[s, :COLS].astype(F32)
            bc_ref[rows, N:] = r_ref[s, COLS : 2 * COLS].astype(F32)
        copies.append(pltpu.make_async_copy(bc_ref.at[at], bc_hbm.at[at], sems.at[i, 0]))
        copies[-1].start()
        steps = jnp.concatenate([unfold_steps(r_ref[s]) for s in part], axis=0)
        dt_ref[:, at] = steps.T[:H]
        copies.append(pltpu.make_async_copy(dt_ref.at[:, at], dt_hbm.at[:, at], sems.at[i, 1]))
        copies[-1].start()
    for copy in copies:
        copy.wait()


def call(kernel, outs, *args, scratch=(), far=False, far_out=False, limit=LIMIT):
    return pl.pallas_call(
        kernel,
        out_shape=[jax.ShapeDtypeStruct(shape, kind) for shape, kind in outs],
        in_specs=[pl.BlockSpec(memory_space=pltpu.HBM if far else pltpu.VMEM)] * len(args),
        out_specs=[pl.BlockSpec(memory_space=pltpu.HBM if far_out else pltpu.VMEM)] * len(outs),
        scratch_shapes=list(scratch),
        compiler_params=pltpu.CompilerParams(vmem_limit_bytes=limit),
    )(*args)


def unpack(w_all):
    return pl.pallas_call(
        unpack_kernel,
        out_shape=[jax.ShapeDtypeStruct((D, 2 * N), F32), jax.ShapeDtypeStruct((H, D), F32)],
        in_specs=[pl.BlockSpec(memory_space=pltpu.VMEM)],
        out_specs=[pl.BlockSpec(memory_space=pltpu.HBM)] * 2,
        scratch_shapes=[
            pltpu.VMEM((D, 2 * N), F32),
            pltpu.VMEM((H, D), F32),
            pltpu.SemaphoreType.DMA((STAGES, 2)),
        ],
        compiler_params=pltpu.CompilerParams(vmem_limit_bytes=LIMIT),
    )(w_all)


def exchange(v, axis):
    return lax.all_to_all(v, axis, split_axis=0, concat_axis=0, tiled=True)


def per_device(hidden, x_input, grad_out, bc_weight, dt_weight, dt_bias, a_log, d_skip):
    prm = jnp.pad(jnp.stack([dt_bias, a_log, d_skip]), ((0, 5), (0, LANES - H)))
    [packed] = call(
        project_kernel,
        [((HEAD, TOKENS, PACK), BF16)],
        hidden, bc_weight, dt_weight.T, x_input, grad_out,
        scratch=[
            pltpu.VMEM((HEAD, TOKENS, PACK), BF16),
            pltpu.VMEM((TOKENS, H * WIDTH), BF16),
            pltpu.VMEM((TOKENS, H * WIDTH), BF16),
            pltpu.VMEM((TOKENS, D), BF16),
            pltpu.VMEM((D, 2 * N), BF16),
            pltpu.VMEM((H, D), BF16),
            pltpu.SemaphoreType.DMA((8,)),
        ],
        far=True,
        far_out=True,
        limit=FULL,
    )
    mine = exchange(packed, "head").reshape(SPAN, PACK)
    [hid_send] = call(slab_kernel, [((SEQ, TOKENS // 2, 3 * LANES), BF16)], hidden)
    [sent] = call(
        totals_kernel, [((SEQ, 2 * SLAB, CH + 3 * LANES), BF16)], mine, prm, hid_send
    )
    totals = exchange(sent, "seq")
    [inner] = call(
        inner_kernel,
        [((SPAN, PACK + LANES), F32)],
        mine, prm,
        scratch=[pltpu.VMEM((SPAN, SPAN), F32)],
    )
    totals, inner = lax.optimization_barrier((totals, inner))
    [states] = call(prefix_kernel, [((SEQ, 2 * SLAB, CH), BF16)], totals)
    states = exchange(states, "seq")
    d_part, both = call(
        carry_kernel,
        [((HEAD, TOKENS, DPACK), BF16), ((SPAN, 2 * CH), BF16)],
        mine, prm, states, inner,
    )
    d_part = exchange(d_part, "head")
    [d_send] = call(
        reduce_kernel,
        [((SEQ, TOKENS, DPACK), BF16)],
        d_part,
    )
    d_all = exchange(d_send, "seq")
    [grad_hidden] = call(
        hidden_kernel, [((TOKENS, D), BF16)], d_send, bc_weight, dt_weight.T
    )
    d_all, grad_hidden = lax.optimization_barrier((d_all, grad_hidden))
    w_part, param_grads = call(
        weight_kernel, [((ROWS, LANES), BF16), ((3, H), F32)], d_all, totals
    )
    for far in (1, 2):
        other = lax.ppermute(w_part, "head", [(i, i ^ far) for i in range(HEAD)])
        [w_part] = call(add_kernel, [((ROWS, LANES), BF16)], w_part, other)
    other = lax.ppermute(w_part, "head", [(i, i ^ 7) for i in range(HEAD)])
    [w_sum] = call(
        spread_kernel,
        [((SEQ, ROWS, LANES), BF16)],
        w_part, other,
        limit=NEAR,
    )
    w_sum, both = lax.optimization_barrier((w_sum, both))
    w_all = exchange(w_sum, "seq")
    blocks = list(call(rotate_kernel, [((TOKENS, 2 * CH), BF16)] * HEAD, both))
    for j, k in enumerate(STEPS):
        if k > 0:
            ring = [(i, (i + k) % HEAD) for i in range(HEAD)]
            blocks[j] = lax.ppermute(blocks[j], "head", ring)
    mixer_out, grad_x = call(
        finish_kernel, [((TOKENS, H * WIDTH), BF16)] * 2, *blocks
    )
    grad_bc_weight, grad_dt_weight = unpack(w_all)
    return (mixer_out, grad_x, grad_hidden, grad_bc_weight, grad_dt_weight.T, param_grads)


def solution(mesh):
    rows = P(("dp", "seq", "head"), None)
    return jax.shard_map(
        per_device,
        mesh=mesh,
        in_specs=(rows, rows, rows, P(), P(), P(), P(), P()),
        out_specs=(rows, rows, rows, P("dp", None), P("dp", None), P("dp", None)),
        check_vma=False,
    )
```
